32 devices in a mesh: seq: 16 (over z, y, core), fsdp: 2 (over x).
Axes of the slice: x: 2, y: 2, z: 4, core: 2. Of those that a mesh axis runs over, the one named last changes fastest.
Arguments:
- cotangent: bfloat16 [2048, 1536], P('seq', 'fsdp'), may hold values from -6 to 6
- out_weight: bfloat16 [1536, 1536], P('fsdp', 'seq'), may hold values from -0.15625 to 0.15625
- values: bfloat16 [2048, 1536], P('seq', 'fsdp'), may hold values from -1.5 to 1.5
- gate_input: bfloat16 [2048, 1536], P('seq', 'fsdp'), may hold values from -6 to 6
- conv_out: bfloat16 [2048, 1536], P('seq', 'fsdp'), may hold values from -6 to 6
- filter_taps: bfloat16 [1536, 2048], P('fsdp'), may hold values from -0.125 to 0.125
Outputs:
- grad_value: bfloat16 [2048, 1536], P('seq', 'fsdp')
- grad_gate: bfloat16 [2048, 1536], P('seq', 'fsdp')
- grad_filter: float32 [2048, 1536], P('seq', 'fsdp')
- grad_weight: float32 [1536, 1536], P('fsdp', 'seq')
The draws below stay inside these ranges and needn't reach their ends.
All inputs are finite; a program needn't handle non-finite values.
Results may differ from the reference program's by a relative error of at most 0.007.
Values may be sent and summed in bfloat16 or wider, within the bound.
A program may use at most 128 MiB of HBM per device.

```python
import jax
import jax.numpy as jnp
from jax import lax

D = 1536
TOK_DEV = 128
SEQ = 2048


def raised(drawn, key, source, target, parts, factor):
    def block_of(dim):
        return (jnp.arange(drawn.shape[dim]) // (drawn.shape[dim] // parts)).reshape((-1,) + (1,) * (drawn.ndim - 1 - dim))

    one_side = jax.random.permutation(key, parts)[block_of(target)]
    far = (block_of(target) + parts // 2) % parts
    return jnp.where((block_of(source) == one_side) | (block_of(source) == far), factor * drawn, drawn)


def block_scale(stream_key, dims, shards, least, high):
    def one(axis_at, blocks):
        steps = jax.random.uniform(jax.random.fold_in(jax.random.fold_in(stream_key, 6), axis_at), (blocks,), jnp.float32, least / len(shards), high / len(shards))
        return jnp.repeat(jnp.exp(steps), dims[axis_at] // blocks).reshape((-1,) + (1,) * (len(dims) - axis_at - 1))

    loudness = one(*shards[0])
    for cut in shards[1:]:
        loudness = loudness * one(*cut)
    return loudness


def scatter_about(stream_key, extent, scale, reach, cuts=(), kind=jnp.bfloat16):
    entries = jax.random.normal(stream_key, extent, jnp.float32) * scale
    if len(cuts) > 0:
        entries = block_scale(stream_key, extent, cuts, -0.22, 0.18) * entries
    return jnp.clip(entries, min=-reach, max=reach).astype(kind)


def heavy_noise(own_key, extent, spread, limit, cuts, heavy, kind=jnp.bfloat16):
    values = spread * jax.random.normal(own_key, extent, jnp.float32)
    if cuts:
        values = values * block_scale(own_key, extent, cuts, -0.22, 0.18)
    return jnp.clip(raised(values, jax.random.fold_in(own_key, 3), *heavy), -limit, limit).astype(kind)


def setup_inputs(seed: int = 0) -> dict:
    key_list = jax.random.split(jax.random.key(seed), 7)
    return {
        "cotangent": heavy_noise(key_list[0], (SEQ, D), 1.0, 6.0, ((0, 16), (1, 2)), (0, 1, 16, 2.0)),
        "out_weight": scatter_about(key_list[1], (D, D), D ** -0.5, 0.15625, ((0, 2), (1, 16))),
        "values": scatter_about(key_list[2], (SEQ, D), 0.25, 1.5, ((0, 16), (1, 2))),
        "gate_input": scatter_about(key_list[3], (SEQ, D), 1.0, 6.0, ((0, 16), (1, 2))),
        "conv_out": scatter_about(key_list[4], (SEQ, D), 1.0, 6.0, ((0, 16), (1, 2))),
        "filter_taps": scatter_about(key_list[5], (D, SEQ), SEQ ** -0.5, 0.125, ((0, 2),)),
    }


def make_tables(block_rows):
    period = 2 * block_rows
    frequency = lax.broadcasted_iota(jnp.int32, (period, period), 0)
    position = lax.broadcasted_iota(jnp.int32, (period, period), 1)
    angles = ((frequency * position) % period).astype(jnp.float32) * (2.0 * jnp.pi / period)
    cosine = jnp.cos(angles)
    sine_part = jnp.sin(angles)
    parity = 1.0 - 2.0 * (position % 2).astype(jnp.float32)
    dft_cos = cosine.astype(jnp.bfloat16)
    dft_sin = (-sine_part).astype(jnp.bfloat16)
    back_cos = (parity * cosine / period).astype(jnp.bfloat16)
    back_sin = (-parity * sine_part / period).astype(jnp.bfloat16)
    return dft_cos, dft_sin, back_cos, back_sin


def high_dot(left, right):
    return jnp.dot(left, right, precision=lax.Precision.HIGHEST, preferred_element_type=jnp.float32)


def round_wide(array):
    narrow = lax.optimization_barrier(array.astype(jnp.bfloat16))
    return narrow.astype(jnp.float32)


def reference(cotangent, out_weight, values, gate_input, conv_out, filter_taps):
    grad_mixed = jnp.dot(cotangent, out_weight.T, preferred_element_type=jnp.float32)
    gate_wide = gate_input.astype(jnp.float32)
    conv_wide = conv_out.astype(jnp.float32)
    grad_gate = (grad_mixed * conv_wide).astype(jnp.bfloat16)
    grad_conv = (grad_mixed * gate_wide).astype(jnp.bfloat16)
    gated = (gate_wide * conv_wide).astype(jnp.bfloat16)
    grad_weight = jnp.dot(gated.T, cotangent, preferred_element_type=jnp.float32)

    block_rows = TOK_DEV
    length, channels = grad_conv.shape
    count = length // block_rows
    period = 2 * block_rows
    dft_cos, dft_sin, back_cos, back_sin = make_tables(block_rows)
    fwd_cos = dft_cos.astype(jnp.float32)
    fwd_sin = dft_sin.astype(jnp.float32)
    inv_cos = back_cos.astype(jnp.float32)
    inv_sin = back_sin.astype(jnp.float32)

    def spectra(whole):
        blocks = whole.astype(jnp.float32).reshape(count, block_rows, channels)
        real_part = jnp.einsum("fb,nbc->nfc", fwd_cos[:, :block_rows], blocks, precision=lax.Precision.HIGHEST)
        imag_part = jnp.einsum("fb,nbc->nfc", fwd_sin[:, :block_rows], blocks, precision=lax.Precision.HIGHEST)
        return real_part, imag_part

    conv_re, conv_im = spectra(grad_conv)
    val_re, val_im = spectra(values)
    zero_blocks = jnp.zeros((count, period, channels), jnp.float32)
    conv_re_pad = jnp.concatenate([conv_re, zero_blocks], axis=0)
    conv_im_pad = jnp.concatenate([conv_im, zero_blocks], axis=0)
    padded_taps = jnp.concatenate([jnp.zeros((channels, block_rows), jnp.float32), filter_taps.astype(jnp.float32)], axis=1)

    def one_offset(carry, offset):
        sum_re, sum_im, lag_buf = carry
        window = lax.dynamic_slice_in_dim(padded_taps, offset * block_rows, period, 1)
        taps_re = high_dot(fwd_cos, window.T)
        taps_im = high_dot(fwd_sin, window.T)
        later_re = lax.dynamic_slice_in_dim(conv_re_pad, offset, count, 0)
        later_im = lax.dynamic_slice_in_dim(conv_im_pad, offset, count, 0)
        mix_re = round_wide(later_re * taps_re + later_im * taps_im)
        mix_im = round_wide(later_re * taps_im - later_im * taps_re)
        sum_re = sum_re + mix_re
        sum_im = sum_im + mix_im
        fil_re = jnp.sum(round_wide(val_re * later_re + val_im * later_im), axis=0)
        fil_im = jnp.sum(round_wide(val_re * later_im - val_im * later_re), axis=0)
        lag_part = high_dot(inv_cos, fil_re) + high_dot(inv_sin, fil_im)
        start = offset * block_rows
        current = lax.dynamic_slice_in_dim(lag_buf, start, period, 0)
        lag_buf = lax.dynamic_update_slice_in_dim(lag_buf, current + lag_part, start, 0)
        return (sum_re, sum_im, lag_buf), None

    init = (jnp.zeros((count, period, channels), jnp.float32), jnp.zeros((count, period, channels), jnp.float32), jnp.zeros(((count + 1) * block_rows, channels), jnp.float32))
    (sum_re, sum_im, lag_buf), _ = lax.scan(one_offset, init, jnp.arange(count, dtype=jnp.int32))
    value_blocks = jnp.einsum("af,nfc->nac", inv_cos[:block_rows], sum_re, precision=lax.Precision.HIGHEST) - jnp.einsum("af,nfc->nac", inv_sin[:block_rows], sum_im, precision=lax.Precision.HIGHEST)
    grad_value = value_blocks.reshape(length, channels).astype(jnp.bfloat16)
    grad_filter = lag_buf[block_rows:]
    return (grad_value, grad_gate, grad_filter.astype(jnp.float32), grad_weight)
```

```python
import functools

import jax
import jax.numpy as jnp
import numpy as np
from jax import lax
from jax.experimental import pallas as pl
from jax.experimental.pallas import tpu as pltpu
from jax.sharding import PartitionSpec as P

MESH = pl.DeviceIdType.MESH


def shifted(block, axis, distance):
    devices = range(lax.axis_size(axis))
    route = [(i - distance, i) for i in devices if i - distance in devices]
    return lax.ppermute(block, axis, route)


def make_tables(block_rows):
    period = 2 * block_rows
    frequency = lax.broadcasted_iota(jnp.int32, (period, period), 0)
    position = lax.broadcasted_iota(jnp.int32, (period, period), 1)
    angles = (frequency * position % period).astype(jnp.float32) * (2.0 * jnp.pi / period)
    cosine = jnp.cos(angles)
    sine_part = jnp.sin(angles)
    parity = 1.0 - 2.0 * (position % 2).astype(jnp.float32)
    dft_cos = cosine.astype(jnp.bfloat16)
    dft_sin = (-sine_part).astype(jnp.bfloat16)
    back_cos = (parity * cosine / period).astype(jnp.bfloat16)
    back_sin = (-parity * sine_part / period).astype(jnp.bfloat16)
    return (dft_cos, dft_sin, back_cos, back_sin)


def narrow_dot(left, right):
    return jnp.dot(left, right, preferred_element_type=jnp.float32)


def product_rows(table, window):
    return lax.dot_general(
        table, window, (((1,), (1,)), ((), ())), preferred_element_type=jnp.float32
    )


def spectrum(block, cos_part, sin_part):
    return (narrow_dot(cos_part, block), narrow_dot(sin_part, block))


def value_term(conv_re, conv_im, filt_re, filt_im, back_table):
    mixed_re = conv_re * filt_re + conv_im * filt_im
    mixed_im = conv_re * filt_im - conv_im * filt_re
    stacked = jnp.concatenate(
        [mixed_re.astype(jnp.bfloat16), mixed_im.astype(jnp.bfloat16)], axis=0
    )
    return narrow_dot(back_table, stacked)


def filter_term(val_re, val_im, conv_re, conv_im, back_table):
    mixed_re = val_re * conv_re + val_im * conv_im
    mixed_im = val_re * conv_im - val_im * conv_re
    stacked = jnp.concatenate(
        [mixed_re.astype(jnp.bfloat16), mixed_im.astype(jnp.bfloat16)], axis=0
    )
    return narrow_dot(back_table, stacked)


def ring_body(cotangent, out_weight, values, gate_input, conv_out, filter_taps):
    block_rows, channels = values.shape
    cycle_size = lax.axis_size("seq")
    weight_rows = lax.all_gather(out_weight, "seq", axis=1, tiled=True)
    features = lax.all_gather(cotangent, "fsdp", axis=1, tiled=True)
    grad_mixed = lax.dot_general(
        features, weight_rows, (((1,), (1,)), ((), ())), preferred_element_type=jnp.float32
    )
    gate_wide = gate_input.astype(jnp.float32)
    conv_wide = conv_out.astype(jnp.float32)
    grad_gate = (grad_mixed * conv_wide).astype(jnp.bfloat16)
    grad_conv = (grad_mixed * gate_wide).astype(jnp.bfloat16)
    gated = (gate_wide * conv_wide).astype(jnp.bfloat16)
    weight_terms = lax.dot_general(
        gated, features, (((0,), (0,)), ((), ())), preferred_element_type=jnp.float32
    )
    grad_weight = lax.psum_scatter(weight_terms, "seq", scatter_dimension=1, tiled=True)
    period = 2 * block_rows
    dft_cos, dft_sin, back_cos, back_sin = make_tables(block_rows)
    block_cos = dft_cos[:, :block_rows]
    block_sin = dft_sin[:, :block_rows]
    value_back = jnp.concatenate([back_cos[:block_rows], -back_sin[:block_rows]], axis=1)
    filter_back = jnp.concatenate([back_cos, back_sin], axis=1)
    padded_taps = jnp.concatenate(
        [jnp.zeros((channels, block_rows), jnp.bfloat16), filter_taps], axis=1
    )
    empty = jnp.zeros((block_rows, channels), jnp.float32)

    def window_spectrum(offset):
        window = lax.dynamic_slice_in_dim(padded_taps, offset * block_rows, period, 1)
        return (product_rows(dft_cos, window), product_rows(dft_sin, window))

    val_re, val_im = spectrum(values, block_cos, block_sin)

    def turn(offset, carry):
        incoming, grad_total, lag_grad = carry
        conv_re, conv_im = spectrum(incoming, block_cos, block_sin)
        filt_re, filt_im = window_spectrum(offset)
        grad_total = grad_total + value_term(conv_re, conv_im, filt_re, filt_im, value_back)
        start = offset * block_rows
        current = lax.dynamic_slice_in_dim(lag_grad, start, period, 0)
        update = current + filter_term(val_re, val_im, conv_re, conv_im, filter_back)
        lag_grad = lax.dynamic_update_slice_in_dim(lag_grad, update, start, 0)
        return (incoming, grad_total, lag_grad)

    def shifted_turn(offset, carry):
        incoming = shifted(carry[0], "seq", -1)
        return turn(offset, (incoming, carry[1], carry[2]))

    lag_zero = jnp.zeros(((cycle_size + 1) * block_rows, channels), jnp.float32)
    carry = turn(0, (grad_conv, empty, lag_zero))
    carry = lax.fori_loop(1, cycle_size, shifted_turn, carry)
    grad_total = carry[1]
    grad_filter = lax.psum_scatter(carry[2][block_rows:], "seq", scatter_dimension=0, tiled=True)
    return (grad_total.astype(jnp.bfloat16), grad_gate, grad_filter, grad_weight)


def packed_tables(rows):
    period = 2 * rows
    freq = np.arange(rows)
    pos = np.arange(period)
    angle = (np.outer(pos, freq) % period) * (2.0 * np.pi / period)
    cosine, sine = np.cos(angle), np.sin(angle)
    alternating = 1.0 - 2.0 * (pos % 2)
    forward_im = -sine
    forward_im[:, 0] = alternating
    forward = np.concatenate([cosine, forward_im], axis=1)
    parity = (1.0 - 2.0 * (freq % 2))[:, None]
    weight = np.where(freq == 0, 1.0, 2.0)[:, None] / period
    back_re = weight * parity * cosine.T
    value_im = weight * parity * sine.T
    lag_im = -value_im
    value_im[0] = alternating / period
    lag_im[0] = alternating / period
    value_back = np.concatenate([back_re, value_im], axis=0)[:, :rows]
    lag_back = np.concatenate([back_re, lag_im], axis=0)
    return tuple(jnp.asarray(t, jnp.bfloat16) for t in (forward, value_back, lag_back))


def mixer_kernel(
    n, nz,
    cot_ref, wt_ref, val_ref, gate_ref, conv_ref, taps_ref, fwd_ref, vback_ref, lback_ref,
    gv_ref, gg_ref, gf_ref, gw_ref,
    feat, wall, gated_all, featq, featr, valt, valr, gct, gcr, gvt, gvr, gft, gfr,
    taps, cre, cim, tre, tim, tmix, vre, vim, vmix, sums, lags, pw, pwr,
    xsem, wzs, wzr, wys, wyr, wcs, wcr, gts, gtr, fts, ftr, vs, vr, cs, cr, os, orr, ls, lr, rs, rr, tsem,
):
    rows = cot_ref.shape[0]
    group = gct.shape[1]
    bf16, f32 = jnp.bfloat16, jnp.float32
    me = lax.axis_index("seq")
    fs = lax.axis_index("fsdp")
    zi, q = me // 4, me % 4
    y, core = q // 2, q % 2
    quad = [
        (1 - y if k >= 2 else y) * 2 + (1 - core if k % 2 else core) for k in range(4)
    ]

    def at(zshift, k):
        return lax.rem(zi + zshift + nz, nz) * 4 + quad[k]

    def send(src, dst, send_sem, recv_sem, seq, fsdp=None):
        return pltpu.make_async_remote_copy(
            src_ref=src, dst_ref=dst, send_sem=send_sem, recv_sem=recv_sem,
            device_id=(seq, fs if fsdp is None else fsdp), device_id_type=MESH,
        )

    barrier = pltpu.get_barrier_semaphore()
    for k in range(1, n):
        pl.semaphore_signal(
            barrier, inc=1, device_id=(lax.rem(me + k, n), fs), device_id_type=MESH
        )
    pl.semaphore_signal(barrier, inc=1, device_id=(me, 1 - fs), device_id_type=MESH)
    pl.semaphore_wait(barrier, n)

    pending = []

    def go(copy):
        copy.start()
        pending.append(copy)
        return copy

    x_copy = go(send(cot_ref, feat.at[fs], xsem.at[0], xsem.at[1], me, 1 - fs))
    for k in range(1, nz):
        go(send(wt_ref, wall.at[me], wzs.at[k], wzr.at[k], at(k, 0)))
    go(send(wt_ref, wall.at[me], wys.at[0], wyr.at[0], at(0, 2)))
    go(send(wt_ref, wall.at[me], wcs.at[0], wcr.at[0], at(0, 1)))
    taps_copy = pltpu.make_async_copy(
        taps_ref.at[pl.ds(pl.multiple_of(me * group, group), group), :],
        taps.at[:, rows:], tsem.at[0],
    )
    taps_copy.start()
    feat[fs] = cot_ref[...]
    wall[me] = wt_ref[...]
    taps[:, :rows] = jnp.zeros((group, rows), bf16)

    def all_to_all(src, dst, send_sems, recv_sems):
        dst[me] = src[me]
        for k in range(1, n):
            to = lax.rem(me + k, n)
            go(send(src.at[to], dst.at[me], send_sems.at[k], recv_sems.at[k], to))

    def arrive(src, dst, send_sems, recv_sems):
        for k in range(1, n):
            origin = lax.rem(me + n - k, n)
            send(src.at[me], dst.at[origin], send_sems.at[k], recv_sems.at[k], origin).wait_recv()

    valt[...] = val_ref[...].astype(f32).T.astype(bf16).reshape(n, group, rows)
    all_to_all(valt, valr, vs, vr)
    gate_wide = gate_ref[...].astype(f32)
    conv_wide = conv_ref[...].astype(f32)
    gated_all[q] = (gate_wide * conv_wide).astype(bf16)
    for k in range(1, 4):
        go(send(gated_all.at[q], gated_all.at[q], gts.at[k], gtr.at[k], at(0, k)))

    for k in range(1, nz):
        slot = wall.at[at(-k, 0)]
        send(wt_ref, slot, wzs.at[k], wzr.at[k], at(k, 0)).wait_recv()
        go(send(slot, slot, wys.at[k], wyr.at[k], at(0, 2)))
        go(send(slot, slot, wcs.at[k], wcr.at[k], at(0, 1)))

    x_copy.wait_recv()
    for part in range(2):
        turned = feat[part].astype(f32).T.astype(bf16)
        per = turned.shape[0] // n * 2
        for j in range(n // 2):
            s = part * (n // 2) + j
            featq[s % 4, s // 4] = turned[j * per:(j + 1) * per]
    featr[q] = featq[q]
    for k in range(1, 4):
        go(send(featq.at[quad[k]], featr.at[q], fts.at[k], ftr.at[k], at(0, k)))

    for k in range(nz):
        slot = wall.at[at(-k, 2)]
        send(slot, slot, wys.at[k], wyr.at[k], at(0, 2)).wait_recv()
        go(send(slot, slot, wcs.at[nz + k], wcr.at[nz + k], at(0, 1)))

    lane = lax.broadcasted_iota(jnp.int32, (group, rows), 1)

    def split(spec, re_ref, im_ref, mix_ref, j, sign):
        real, imag = spec[:, :rows], spec[:, rows:]
        re_ref[j] = real
        if mix_ref is None:
            im_ref[j] = imag
        else:
            im_ref[j] = jnp.where(lane == 0, 0.0, imag)
            mix_ref[j] = jnp.where(lane == 0, sign * imag, real)

    def spectra(source, re_ref, im_ref, mix_ref):
        def one(j, carry):
            spec = jnp.dot(source[j], fwd_ref[:rows, :], preferred_element_type=f32)
            split(spec, re_ref, im_ref, mix_ref, j, 1.0)
            return carry
        lax.fori_loop(0, n, one, 0, unroll=4)

    taps_copy.wait()
    for m in range(n):
        spec = jnp.dot(
            taps[:, m * rows:(m + 2) * rows], fwd_ref[...], preferred_element_type=f32
        )
        split(spec, tre, tim, tmix, m, -1.0)
    arrive(valt, valr, vs, vr)
    spectra(valr, vre, vim, vmix)

    for k in range(2 * nz):
        slot = wall.at[at(-(k % nz), 1 if k < nz else 3)]
        send(slot, slot, wcs.at[k], wcr.at[k], at(0, 1)).wait_recv()
    half = n // 2
    width = wall.shape[2]
    mixed = jnp.dot(
        feat[0], wall[:half].reshape(-1, width), preferred_element_type=f32
    ) + jnp.dot(feat[1], wall[half:].reshape(-1, width), preferred_element_type=f32)
    gg_ref[...] = (mixed * conv_ref[...].astype(f32)).astype(bf16)
    gct[...] = (mixed * gate_ref[...].astype(f32)).T.astype(bf16).reshape(n, group, rows)
    all_to_all(gct, gcr, cs, cr)

    for k in range(1, 4):
        send(gated_all.at[q], gated_all.at[quad[k]], gts.at[k], gtr.at[k], at(0, k)).wait_recv()
        send(featq.at[q], featr.at[quad[k]], fts.at[k], ftr.at[k], at(0, k)).wait_recv()
    for zz in range(nz):
        part = jnp.dot(featr[0, zz], gated_all[0], preferred_element_type=f32)
        for k in range(1, 4):
            part = part + jnp.dot(featr[k, zz], gated_all[k], preferred_element_type=f32)
        pw[zz] = part.astype(bf16)

        @pl.when(zz == zi)
        def _():
            gw_ref[...] = part

    for k in range(1, nz):
        to = lax.rem(zi + k, nz)
        go(send(pw.at[to], pwr.at[k - 1], rs.at[k], rr.at[k], at(k, 0)))

    arrive(gct, gcr, cs, cr)
    spectra(gcr, cre, cim, None)

    def value_rows(r, carry):
        at_rows = pl.ds(pl.multiple_of(r * 8, 8), 8)
        for i in range(n):
            c_re, c_im = cre[i:n, at_rows, :], cim[i:n, at_rows, :]
            t_re, t_im = tre[:n - i, at_rows, :], tim[:n - i, at_rows, :]
            t_mix = tmix[:n - i, at_rows, :]
            sums[i, at_rows, :rows] = jnp.sum(c_re * t_re + c_im * t_im, axis=0)
            sums[i, at_rows, rows:] = jnp.sum(c_re * t_im - c_im * t_mix, axis=0)
        return carry

    lax.fori_loop(0, group // 8, value_rows, 0)
    packed = sums[...].astype(bf16).reshape(n * group, 2 * rows)
    blocks = jnp.dot(packed, vback_ref[...], preferred_element_type=f32)
    gvt[...] = blocks.astype(bf16).reshape(n, group, rows)
    all_to_all(gvt, gvr, os, orr)

    def lag_rows(r, carry):
        at_rows = pl.ds(pl.multiple_of(r * 8, 8), 8)
        for m in range(n):
            c_re, c_im = cre[m:n, at_rows, :], cim[m:n, at_rows, :]
            v_re, v_im = vre[:n - m, at_rows, :], vim[:n - m, at_rows, :]
            v_mix = vmix[:n - m, at_rows, :]
            lags[m, at_rows, :rows] = jnp.sum(v_re * c_re + v_im * c_im, axis=0)
            lags[m, at_rows, rows:] = jnp.sum(v_mix * c_im - v_im * c_re, axis=0)
        return carry

    lax.fori_loop(0, group // 8, lag_rows, 0)
    packed = lags[...].astype(bf16).reshape(n * group, 2 * rows)
    parts = jnp.dot(packed, lback_ref[...], preferred_element_type=f32)
    first = jnp.concatenate([parts[group:, :rows], jnp.zeros((group, rows), f32)], axis=0)
    gft[...] = (parts[:, rows:] + first).astype(bf16).reshape(n, group, rows)
    all_to_all(gft, gfr, ls, lr)

    for k in range(1, nz):
        send(pw.at[0], pwr.at[k - 1], rs.at[k], rr.at[k], at(k, 0)).wait_recv()
        gw_ref[...] += pwr[k - 1].astype(f32)
    arrive(gvt, gvr, os, orr)
    gv_ref[...] = gvr[...].reshape(n * group, rows)
    arrive(gft, gfr, ls, lr)
    gf_ref[...] = gfr[...].reshape(n * group, rows).astype(f32)
    for copy in pending:
        copy.wait_send()


def split_body(cotangent, out_weight, values, gate_input, conv_out, filter_taps):
    rows, channels = values.shape
    n = lax.axis_size("seq")
    nz = n // 4
    group = channels // n
    slice_cols = out_weight.shape[1]
    forward, value_back, lag_back = packed_tables(rows)
    bf16, f32 = jnp.bfloat16, jnp.float32
    vm = pltpu.VMEM
    dma = pltpu.SemaphoreType.DMA
    trip = (n, group, rows)
    vmem = pl.BlockSpec(memory_space=pltpu.VMEM)
    gv, gg, gf, gw = pl.pallas_call(
        functools.partial(mixer_kernel, n, nz),
        out_shape=(
            jax.ShapeDtypeStruct((channels, rows), bf16),
            jax.ShapeDtypeStruct((rows, channels), bf16),
            jax.ShapeDtypeStruct((channels, rows), f32),
            jax.ShapeDtypeStruct((slice_cols, channels), f32),
        ),
        in_specs=[vmem] * 5 + [pl.BlockSpec(memory_space=pl.ANY)] + [vmem] * 3,
        out_specs=(vmem,) * 4,
        scratch_shapes=[
            vm((2, rows, channels), bf16),
            vm((n, slice_cols, channels), bf16),
            vm((4, rows, channels), bf16),
            vm((4, nz, slice_cols, rows), bf16),
            vm((4, nz, slice_cols, rows), bf16),
        ] + [vm(trip, bf16)] * 8 + [
            vm((group, (n + 1) * rows), bf16),
        ] + [vm(trip, f32)] * 8 + [
            vm((n, group, 2 * rows), f32),
            vm((n, group, 2 * rows), f32),
            vm((nz, slice_cols, channels), bf16),
            vm((nz - 1, slice_cols, channels), bf16),
            dma((2,)),
            dma((nz,)), dma((nz,)), dma((nz,)), dma((nz,)), dma((2 * nz,)), dma((2 * nz,)),
            dma((4,)), dma((4,)), dma((4,)), dma((4,)),
        ] + [dma((n,))] * 8 + [dma((nz,)), dma((nz,)), dma((1,))],
        compiler_params=pltpu.CompilerParams(
            collective_id=0, has_side_effects=True, vmem_limit_bytes=48 * 1024 * 1024
        ),
    )(
        cotangent, out_weight.T, values, gate_input, conv_out, filter_taps,
        forward, value_back, lag_back,
    )
    return gv.T, gg, gf.T, gw.T


def solution(mesh):
    in_specs = (
        P("seq", "fsdp"),
        P("fsdp", "seq"),
        P("seq", "fsdp"),
        P("seq", "fsdp"),
        P("seq", "fsdp"),
        P("fsdp", None),
    )
    out_specs = (P("seq", "fsdp"), P("seq", "fsdp"), P("seq", "fsdp"), P("fsdp", "seq"))

    def body(*blocks):
        rows, channels = blocks[2].shape
        n = mesh.shape["seq"]
        aligned = rows % 128 == 0 and channels % (16 * n) == 0 and blocks[1].shape[1] % 16 == 0
        if aligned and n % 8 == 0 and mesh.shape["fsdp"] == 2:
            return split_body(*blocks)
        return ring_body(*blocks)

    return jax.shard_map(body, mesh=mesh, in_specs=in_specs, out_specs=out_specs, check_vma=False)
```

```python
import functools

import jax
import jax.numpy as jnp
import numpy as np
from jax import lax
from jax.experimental import pallas as pl
from jax.experimental.pallas import tpu as pltpu
from jax.sharding import PartitionSpec as P

MESH = pl.DeviceIdType.MESH


def shifted(block, axis, distance):
    devices = range(lax.axis_size(axis))
    route = [(i - distance, i) for i in devices if i - distance in devices]
    return lax.ppermute(block, axis, route)


def make_tables(block_rows):
    period = 2 * block_rows
    frequency = lax.broadcasted_iota(jnp.int32, (period, period), 0)
    position = lax.broadcasted_iota(jnp.int32, (period, period), 1)
    angles = (frequency * position % period).astype(jnp.float32) * (2.0 * jnp.pi / period)
    cosine = jnp.cos(angles)
    sine_part = jnp.sin(angles)
    parity = 1.0 - 2.0 * (position % 2).astype(jnp.float32)
    dft_cos = cosine.astype(jnp.bfloat16)
    dft_sin = (-sine_part).astype(jnp.bfloat16)
    back_cos = (parity * cosine / period).astype(jnp.bfloat16)
    back_sin = (-parity * sine_part / period).astype(jnp.bfloat16)
    return (dft_cos, dft_sin, back_cos, back_sin)


def narrow_dot(left, right):
    return jnp.dot(left, right, preferred_element_type=jnp.float32)


def product_rows(table, window):
    return lax.dot_general(
        table, window, (((1,), (1,)), ((), ())), preferred_element_type=jnp.float32
    )


def spectrum(block, cos_part, sin_part):
    return (narrow_dot(cos_part, block), narrow_dot(sin_part, block))


def value_term(conv_re, conv_im, filt_re, filt_im, back_table):
    mixed_re = conv_re * filt_re + conv_im * filt_im
    mixed_im = conv_re * filt_im - conv_im * filt_re
    stacked = jnp.concatenate(
        [mixed_re.astype(jnp.bfloat16), mixed_im.astype(jnp.bfloat16)], axis=0
    )
    return narrow_dot(back_table, stacked)


def filter_term(val_re, val_im, conv_re, conv_im, back_table):
    mixed_re = val_re * conv_re + val_im * conv_im
    mixed_im = val_re * conv_im - val_im * conv_re
    stacked = jnp.concatenate(
        [mixed_re.astype(jnp.bfloat16), mixed_im.astype(jnp.bfloat16)], axis=0
    )
    return narrow_dot(back_table, stacked)


def ring_body(cotangent, out_weight, values, gate_input, conv_out, filter_taps):
    block_rows, channels = values.shape
    cycle_size = lax.axis_size("seq")
    weight_rows = lax.all_gather(out_weight, "seq", axis=1, tiled=True)
    features = lax.all_gather(cotangent, "fsdp", axis=1, tiled=True)
    grad_mixed = lax.dot_general(
        features, weight_rows, (((1,), (1,)), ((), ())), preferred_element_type=jnp.float32
    )
    gate_wide = gate_input.astype(jnp.float32)
    conv_wide = conv_out.astype(jnp.float32)
    grad_gate = (grad_mixed * conv_wide).astype(jnp.bfloat16)
    grad_conv = (grad_mixed * gate_wide).astype(jnp.bfloat16)
    gated = (gate_wide * conv_wide).astype(jnp.bfloat16)
    weight_terms = lax.dot_general(
        gated, features, (((0,), (0,)), ((), ())), preferred_element_type=jnp.float32
    )
    grad_weight = lax.psum_scatter(weight_terms, "seq", scatter_dimension=1, tiled=True)
    period = 2 * block_rows
    dft_cos, dft_sin, back_cos, back_sin = make_tables(block_rows)
    block_cos = dft_cos[:, :block_rows]
    block_sin = dft_sin[:, :block_rows]
    value_back = jnp.concatenate([back_cos[:block_rows], -back_sin[:block_rows]], axis=1)
    filter_back = jnp.concatenate([back_cos, back_sin], axis=1)
    padded_taps = jnp.concatenate(
        [jnp.zeros((channels, block_rows), jnp.bfloat16), filter_taps], axis=1
    )
    empty = jnp.zeros((block_rows, channels), jnp.float32)

    def window_spectrum(offset):
        window = lax.dynamic_slice_in_dim(padded_taps, offset * block_rows, period, 1)
        return (product_rows(dft_cos, window), product_rows(dft_sin, window))

    val_re, val_im = spectrum(values, block_cos, block_sin)

    def turn(offset, carry):
        incoming, grad_total, lag_grad = carry
        conv_re, conv_im = spectrum(incoming, block_cos, block_sin)
        filt_re, filt_im = window_spectrum(offset)
        grad_total = grad_total + value_term(conv_re, conv_im, filt_re, filt_im, value_back)
        start = offset * block_rows
        current = lax.dynamic_slice_in_dim(lag_grad, start, period, 0)
        update = current + filter_term(val_re, val_im, conv_re, conv_im, filter_back)
        lag_grad = lax.dynamic_update_slice_in_dim(lag_grad, update, start, 0)
        return (incoming, grad_total, lag_grad)

    def shifted_turn(offset, carry):
        incoming = shifted(carry[0], "seq", -1)
        return turn(offset, (incoming, carry[1], carry[2]))

    lag_zero = jnp.zeros(((cycle_size + 1) * block_rows, channels), jnp.float32)
    carry = turn(0, (grad_conv, empty, lag_zero))
    carry = lax.fori_loop(1, cycle_size, shifted_turn, carry)
    grad_total = carry[1]
    grad_filter = lax.psum_scatter(carry[2][block_rows:], "seq", scatter_dimension=0, tiled=True)
    return (grad_total.astype(jnp.bfloat16), grad_gate, grad_filter, grad_weight)


def packed_tables(rows):
    period = 2 * rows
    freq = np.arange(rows)
    pos = np.arange(period)
    angle = (np.outer(pos, freq) % period) * (2.0 * np.pi / period)
    cosine, sine = np.cos(angle), np.sin(angle)
    alternating = 1.0 - 2.0 * (pos % 2)
    forward_im = -sine
    forward_im[:, 0] = alternating
    forward = np.concatenate([cosine, forward_im], axis=1)
    parity = (1.0 - 2.0 * (freq % 2))[:, None]
    weight = np.where(freq == 0, 1.0, 2.0)[:, None] / period
    back_re = weight * parity * cosine.T
    value_im = weight * parity * sine.T
    lag_im = -value_im
    value_im[0] = alternating / period
    lag_im[0] = alternating / period
    value_back = np.concatenate([back_re, value_im], axis=0)[:, :rows]
    lag_back = np.concatenate([back_re, lag_im], axis=0)
    return tuple(jnp.asarray(t, jnp.bfloat16) for t in (forward, value_back, lag_back))


def mixer_kernel(
    n, nz,
    cot_ref, wt_ref, val_ref, gate_ref, conv_ref, taps_ref, fwd_hbm, vback_hbm, lback_hbm,
    gv_ref, gg_ref, gf_ref, gw_ref,
    val_in, gate_in, conv_in, fwd_ref, vback_ref, lback_ref,
    feat, wall, gated_all, featq, featr, valt, valr, gct, gcr, gvt, gvr, gft, gfr,
    taps, cre, cim, tre, tim, tmix, vre, vim, vmix, sums, lags, pw, pair_out, pair_in, cross_out, cross_in,
    xsem, wzs, wzr, wys, wyr, wcs, wcr, gts, gtr, fts, ftr, vs, vr, cs, cr, os, orr, ls, lr, rs, rr, tsem,
):
    rows = val_in.shape[0]
    group = gct.shape[1]
    bf16, f32 = jnp.bfloat16, jnp.float32
    me = lax.axis_index("seq")
    fs = lax.axis_index("fsdp")
    zi, q = me // 4, me % 4
    y, core = q // 2, q % 2
    quad = [
        (1 - y if k >= 2 else y) * 2 + (1 - core if k % 2 else core) for k in range(4)
    ]
    pair = zi + 1 - 2 * (zi % 2)
    cross = lax.rem(zi + 2, 4)
    far = lax.rem(pair + 2, 4)
    levels = [zi, cross, pair, far]

    def at(level, k):
        return levels[level] * 4 + quad[k]

    def send(src, dst, send_sem, recv_sem, seq, fsdp=None):
        return pltpu.make_async_remote_copy(
            src_ref=src, dst_ref=dst, send_sem=send_sem, recv_sem=recv_sem,
            device_id=(seq, fs if fsdp is None else fsdp), device_id_type=MESH,
        )

    local = [
        pltpu.make_async_copy(src, dst, tsem.at[i]) for i, (src, dst) in enumerate([
            (wt_ref, wall.at[me]),
            (cot_ref, feat.at[fs]),
            (gate_ref, gate_in),
            (conv_ref, conv_in),
            (val_ref, val_in),
            (taps_ref.at[pl.ds(pl.multiple_of(me * group, group), group), :], taps.at[:, rows:]),
            (fwd_hbm, fwd_ref),
            (vback_hbm, vback_ref),
            (lback_hbm, lback_ref),
        ])
    ]
    for copy in local:
        copy.start()

    barrier = pltpu.get_barrier_semaphore()
    for k in range(1, n):
        pl.semaphore_signal(
            barrier, inc=1, device_id=(lax.rem(me + k, n), fs), device_id_type=MESH
        )
    pl.semaphore_signal(barrier, inc=1, device_id=(me, 1 - fs), device_id_type=MESH)
    taps[:, :rows] = jnp.zeros((group, rows), bf16)
    pl.semaphore_wait(barrier, n)

    pending = []

    def go(copy):
        copy.start()
        pending.append(copy)
        return copy

    own = wall.at[me]
    go(send(wt_ref, own, wzs.at[1], wzr.at[1], at(1, 0)))
    go(send(wt_ref, own, wzs.at[2], wzr.at[2], at(2, 0)))
    go(send(wt_ref, own, wys.at[0], wyr.at[0], at(0, 2)))
    x_copy = go(send(cot_ref, feat.at[fs], xsem.at[0], xsem.at[1], me, 1 - fs))
    go(send(wt_ref, own, wcs.at[0], wcr.at[0], at(0, 1)))

    def all_to_all(src, dst, send_sems, recv_sems):
        dst[me] = src[me]
        for k in range(1, n):
            to = lax.rem(me + k, n)
            go(send(src.at[to], dst.at[me], send_sems.at[k], recv_sems.at[k], to))

    def arrive(src, dst, send_sems, recv_sems):
        for k in range(1, n):
            origin = lax.rem(me + n - k, n)
            send(src.at[me], dst.at[origin], send_sems.at[k], recv_sems.at[k], origin).wait_recv()

    for copy in local:
        copy.wait()
    gated_all[q] = (gate_in[...].astype(f32) * conv_in[...].astype(f32)).astype(bf16)
    go(send(gated_all.at[q], gated_all.at[q], gts.at[1], gtr.at[1], at(0, 1)))
    valt[...] = val_in[...].astype(f32).T.astype(bf16).reshape(n, group, rows)

    def weight_from(level):
        slot = wall.at[at(level, 0)]
        send(slot, slot, wzs.at[level], wzr.at[level], at(level, 0)).wait_recv()
        if level == 1:
            go(send(slot, slot, wzs.at[3], wzr.at[3], at(2, 0)))
        go(send(slot, slot, wys.at[level], wyr.at[level], at(0, 2)))
        go(send(slot, slot, wcs.at[level], wcr.at[level], at(0, 1)))

    weight_from(1)
    weight_from(2)

    lane = lax.broadcasted_iota(jnp.int32, (group, rows), 1)

    def split(spec, re_ref, im_ref, mix_ref, j, sign):
        real, imag = spec[:, :rows], spec[:, rows:]
        re_ref[j] = real
        if mix_ref is None:
            im_ref[j] = imag
        else:
            im_ref[j] = jnp.where(lane == 0, 0.0, imag)
            mix_ref[j] = jnp.where(lane == 0, sign * imag, real)

    def spectra(source, re_ref, im_ref, mix_ref):
        def one(j, carry):
            spec = jnp.dot(source[j], fwd_ref[:rows, :], preferred_element_type=f32)
            split(spec, re_ref, im_ref, mix_ref, j, 1.0)
            return carry
        lax.fori_loop(0, n, one, 0, unroll=4)

    for m in range(n):
        spec = jnp.dot(
            taps[:, m * rows:(m + 2) * rows], fwd_ref[...], preferred_element_type=f32
        )
        split(spec, tre, tim, tmix, m, -1.0)

    weight_from(3)
    all_to_all(valt, valr, vs, vr)
    go(send(gated_all.at[q], gated_all.at[q], gts.at[2], gtr.at[2], at(0, 2)))

    x_copy.wait_recv()
    for part in range(2):
        turned = feat[part].astype(f32).T.astype(bf16)
        per = turned.shape[0] // n * 2
        for j in range(n // 2):
            s = part * (n // 2) + j
            featq[s % 4, s // 4] = turned[j * per:(j + 1) * per]
    featr[q] = featq[q]
    for k in range(1, 4):
        go(send(featq.at[quad[k]], featr.at[q], fts.at[k], ftr.at[k], at(0, k)))

    for level in range(nz):
        slot = wall.at[at(level, 2)]
        send(slot, slot, wys.at[level], wyr.at[level], at(0, 2)).wait_recv()
        go(send(slot, slot, wcs.at[nz + level], wcr.at[nz + level], at(0, 1)))
    far_gated = gated_all.at[quad[2]]
    send(far_gated, far_gated, gts.at[2], gtr.at[2], at(0, 2)).wait_recv()
    go(send(far_gated, far_gated, gts.at[3], gtr.at[3], at(0, 1)))
    for k in range(2 * nz):
        slot = wall.at[at(k % nz, 1 if k < nz else 3)]
        send(slot, slot, wcs.at[k], wcr.at[k], at(0, 1)).wait_recv()

    half = n // 2
    width = wall.shape[2]
    mixed = jnp.dot(
        feat[0], wall[:half].reshape(-1, width), preferred_element_type=f32
    ) + jnp.dot(feat[1], wall[half:].reshape(-1, width), preferred_element_type=f32)
    gct[...] = (mixed * gate_in[...].astype(f32)).T.astype(bf16).reshape(n, group, rows)
    all_to_all(gct, gcr, cs, cr)
    gg_ref[...] = (mixed * conv_in[...].astype(f32)).astype(bf16)

    for k in range(1, 4):
        there = gated_all.at[quad[k]]
        if k != 2:
            send(there, there, gts.at[k], gtr.at[k], at(0, k)).wait_recv()
        send(featq.at[q], featr.at[quad[k]], fts.at[k], ftr.at[k], at(0, k)).wait_recv()

    def weight_part(level):
        z = levels[level]
        total = jnp.dot(featr[0, z], gated_all[0], preferred_element_type=f32)
        for k in range(1, 4):
            total = total + jnp.dot(featr[k, z], gated_all[k], preferred_element_type=f32)
        return total

    pair_out[0] = weight_part(3).astype(bf16)
    go(send(pair_out.at[0], pair_in.at[0], rs.at[0], rr.at[0], at(2, 0)))
    pair_out[1] = weight_part(2).astype(bf16)
    go(send(pair_out.at[1], pair_in.at[1], rs.at[1], rr.at[1], at(2, 0)))
    pw[0] = weight_part(1)
    pw[1] = weight_part(0)

    arrive(valt, valr, vs, vr)
    spectra(valr, vre, vim, vmix)
    arrive(gct, gcr, cs, cr)
    spectra(gcr, cre, cim, None)

    def value_rows(r, carry):
        at_rows = pl.ds(pl.multiple_of(r * 8, 8), 8)
        for i in range(n):
            c_re, c_im = cre[i:n, at_rows, :], cim[i:n, at_rows, :]
            t_re, t_im = tre[:n - i, at_rows, :], tim[:n - i, at_rows, :]
            t_mix = tmix[:n - i, at_rows, :]
            sums[i, at_rows, :rows] = jnp.sum(c_re * t_re + c_im * t_im, axis=0)
            sums[i, at_rows, rows:] = jnp.sum(c_re * t_im - c_im * t_mix, axis=0)
        return carry

    lax.fori_loop(0, group // 8, value_rows, 0)
    packed = sums[...].astype(bf16).reshape(n * group, 2 * rows)
    blocks = jnp.dot(packed, vback_ref[...], preferred_element_type=f32)
    gvt[...] = blocks.astype(bf16).reshape(n, group, rows)
    all_to_all(gvt, gvr, os, orr)

    send(pair_out.at[0], pair_in.at[0], rs.at[0], rr.at[0], at(2, 0)).wait_recv()
    cross_out[...] = (pw[0] + pair_in[0].astype(f32)).astype(bf16)
    go(send(cross_out, cross_in, rs.at[2], rr.at[2], at(1, 0)))

    def lag_rows(r, carry):
        at_rows = pl.ds(pl.multiple_of(r * 8, 8), 8)
        for m in range(n):
            c_re, c_im = cre[m:n, at_rows, :], cim[m:n, at_rows, :]
            v_re, v_im = vre[:n - m, at_rows, :], vim[:n - m, at_rows, :]
            v_mix = vmix[:n - m, at_rows, :]
            lags[m, at_rows, :rows] = jnp.sum(v_re * c_re + v_im * c_im, axis=0)
            lags[m, at_rows, rows:] = jnp.sum(v_mix * c_im - v_im * c_re, axis=0)
        return carry

    lax.fori_loop(0, group // 8, lag_rows, 0)
    packed = lags[...].astype(bf16).reshape(n * group, 2 * rows)
    parts = jnp.dot(packed, lback_ref[...], preferred_element_type=f32)
    first = jnp.concatenate([parts[group:, :rows], jnp.zeros((group, rows), f32)], axis=0)
    gft[...] = (parts[:, rows:] + first).astype(bf16).reshape(n, group, rows)
    all_to_all(gft, gfr, ls, lr)

    send(pair_out.at[1], pair_in.at[1], rs.at[1], rr.at[1], at(2, 0)).wait_recv()
    send(cross_out, cross_in, rs.at[2], rr.at[2], at(1, 0)).wait_recv()
    gw_ref[...] = pw[1] + pair_in[1].astype(f32) + cross_in[...].astype(f32)
    arrive(gvt, gvr, os, orr)
    gv_ref[...] = gvr[...].reshape(n * group, rows)
    arrive(gft, gfr, ls, lr)
    gf_ref[...] = gfr[...].reshape(n * group, rows).astype(f32)
    for copy in pending:
        copy.wait_send()


def split_body(cotangent, out_weight, values, gate_input, conv_out, filter_taps):
    rows, channels = values.shape
    n = lax.axis_size("seq")
    nz = n // 4
    group = channels // n
    slice_cols = out_weight.shape[1]
    forward, value_back, lag_back = packed_tables(rows)
    bf16, f32 = jnp.bfloat16, jnp.float32
    vm = pltpu.VMEM
    dma = pltpu.SemaphoreType.DMA
    trip = (n, group, rows)
    vmem = pl.BlockSpec(memory_space=pltpu.VMEM)
    gv, gg, gf, gw = pl.pallas_call(
        functools.partial(mixer_kernel, n, nz),
        out_shape=(
            jax.ShapeDtypeStruct((channels, rows), bf16),
            jax.ShapeDtypeStruct((rows, channels), bf16),
            jax.ShapeDtypeStruct((channels, rows), f32),
            jax.ShapeDtypeStruct((slice_cols, channels), f32),
        ),
        in_specs=[pl.BlockSpec(memory_space=pltpu.HBM)] * 9,
        out_specs=(vmem,) * 4,
        scratch_shapes=[vm((rows, channels), bf16)] * 3 + [
            vm((2 * rows, 2 * rows), bf16),
            vm((2 * rows, rows), bf16),
            vm((2 * rows, 2 * rows), bf16),
            vm((2, rows, channels), bf16),
            vm((n, slice_cols, channels), bf16),
            vm((4, rows, channels), bf16),
            vm((4, nz, slice_cols, rows), bf16),
            vm((4, nz, slice_cols, rows), bf16),
        ] + [vm(trip, bf16)] * 8 + [
            vm((group, (n + 1) * rows), bf16),
        ] + [vm(trip, f32)] * 8 + [
            vm((n, group, 2 * rows), f32),
            vm((n, group, 2 * rows), f32),
            vm((2, slice_cols, channels), f32),
            vm((2, slice_cols, channels), bf16),
            vm((2, slice_cols, channels), bf16),
            vm((slice_cols, channels), bf16),
            vm((slice_cols, channels), bf16),
            dma((2,)),
            dma((nz,)), dma((nz,)), dma((nz,)), dma((nz,)), dma((2 * nz,)), dma((2 * nz,)),
            dma((4,)), dma((4,)), dma((4,)), dma((4,)),
        ] + [dma((n,))] * 8 + [dma((3,)), dma((3,)), dma((9,))],
        compiler_params=pltpu.CompilerParams(
            collective_id=0, has_side_effects=True, vmem_limit_bytes=48 * 1024 * 1024
        ),
    )(
        cotangent, out_weight.T, values, gate_input, conv_out, filter_taps,
        forward, value_back, lag_back,
    )
    return gv.T, gg, gf.T, gw.T


def solution(mesh):
    in_specs = (
        P("seq", "fsdp"),
        P("fsdp", "seq"),
        P("seq", "fsdp"),
        P("seq", "fsdp"),
        P("seq", "fsdp"),
        P("fsdp", None),
    )
    out_specs = (P("seq", "fsdp"), P("seq", "fsdp"), P("seq", "fsdp"), P("fsdp", "seq"))

    def body(*blocks):
        rows, channels = blocks[2].shape
        n = mesh.shape["seq"]
        aligned = rows % 128 == 0 and channels % (16 * n) == 0 and blocks[1].shape[1] % 16 == 0
        if aligned and n == 16 and mesh.shape["fsdp"] == 2:
            return split_body(*blocks)
        return ring_body(*blocks)

    return jax.shard_map(body, mesh=mesh, in_specs=in_specs, out_specs=out_specs, check_vma=False)
```

```python
import functools

import jax
import jax.numpy as jnp
import numpy as np
from jax import lax
from jax.experimental import pallas as pl
from jax.experimental.pallas import tpu as pltpu
from jax.sharding import PartitionSpec as P

MESH = pl.DeviceIdType.MESH


def shifted(block, axis, distance):
    devices = range(lax.axis_size(axis))
    route = [(i - distance, i) for i in devices if i - distance in devices]
    return lax.ppermute(block, axis, route)


def make_tables(block_rows):
    period = 2 * block_rows
    frequency = lax.broadcasted_iota(jnp.int32, (period, period), 0)
    position = lax.broadcasted_iota(jnp.int32, (period, period), 1)
    angles = (frequency * position % period).astype(jnp.float32) * (2.0 * jnp.pi / period)
    cosine = jnp.cos(angles)
    sine_part = jnp.sin(angles)
    parity = 1.0 - 2.0 * (position % 2).astype(jnp.float32)
    dft_cos = cosine.astype(jnp.bfloat16)
    dft_sin = (-sine_part).astype(jnp.bfloat16)
    back_cos = (parity * cosine / period).astype(jnp.bfloat16)
    back_sin = (-parity * sine_part / period).astype(jnp.bfloat16)
    return (dft_cos, dft_sin, back_cos, back_sin)


def narrow_dot(left, right):
    return jnp.dot(left, right, preferred_element_type=jnp.float32)


def product_rows(table, window):
    return lax.dot_general(
        table, window, (((1,), (1,)), ((), ())), preferred_element_type=jnp.float32
    )


def spectrum(block, cos_part, sin_part):
    return (narrow_dot(cos_part, block), narrow_dot(sin_part, block))


def value_term(conv_re, conv_im, filt_re, filt_im, back_table):
    mixed_re = conv_re * filt_re + conv_im * filt_im
    mixed_im = conv_re * filt_im - conv_im * filt_re
    stacked = jnp.concatenate(
        [mixed_re.astype(jnp.bfloat16), mixed_im.astype(jnp.bfloat16)], axis=0
    )
    return narrow_dot(back_table, stacked)


def filter_term(val_re, val_im, conv_re, conv_im, back_table):
    mixed_re = val_re * conv_re + val_im * conv_im
    mixed_im = val_re * conv_im - val_im * conv_re
    stacked = jnp.concatenate(
        [mixed_re.astype(jnp.bfloat16), mixed_im.astype(jnp.bfloat16)], axis=0
    )
    return narrow_dot(back_table, stacked)


def ring_body(cotangent, out_weight, values, gate_input, conv_out, filter_taps):
    block_rows, channels = values.shape
    cycle_size = lax.axis_size("seq")
    weight_rows = lax.all_gather(out_weight, "seq", axis=1, tiled=True)
    features = lax.all_gather(cotangent, "fsdp", axis=1, tiled=True)
    grad_mixed = lax.dot_general(
        features, weight_rows, (((1,), (1,)), ((), ())), preferred_element_type=jnp.float32
    )
    gate_wide = gate_input.astype(jnp.float32)
    conv_wide = conv_out.astype(jnp.float32)
    grad_gate = (grad_mixed * conv_wide).astype(jnp.bfloat16)
    grad_conv = (grad_mixed * gate_wide).astype(jnp.bfloat16)
    gated = (gate_wide * conv_wide).astype(jnp.bfloat16)
    weight_terms = lax.dot_general(
        gated, features, (((0,), (0,)), ((), ())), preferred_element_type=jnp.float32
    )
    grad_weight = lax.psum_scatter(weight_terms, "seq", scatter_dimension=1, tiled=True)
    period = 2 * block_rows
    dft_cos, dft_sin, back_cos, back_sin = make_tables(block_rows)
    block_cos = dft_cos[:, :block_rows]
    block_sin = dft_sin[:, :block_rows]
    value_back = jnp.concatenate([back_cos[:block_rows], -back_sin[:block_rows]], axis=1)
    filter_back = jnp.concatenate([back_cos, back_sin], axis=1)
    padded_taps = jnp.concatenate(
        [jnp.zeros((channels, block_rows), jnp.bfloat16), filter_taps], axis=1
    )
    empty = jnp.zeros((block_rows, channels), jnp.float32)

    def window_spectrum(offset):
        window = lax.dynamic_slice_in_dim(padded_taps, offset * block_rows, period, 1)
        return (product_rows(dft_cos, window), product_rows(dft_sin, window))

    val_re, val_im = spectrum(values, block_cos, block_sin)

    def turn(offset, carry):
        incoming, grad_total, lag_grad = carry
        conv_re, conv_im = spectrum(incoming, block_cos, block_sin)
        filt_re, filt_im = window_spectrum(offset)
        grad_total = grad_total + value_term(conv_re, conv_im, filt_re, filt_im, value_back)
        start = offset * block_rows
        current = lax.dynamic_slice_in_dim(lag_grad, start, period, 0)
        update = current + filter_term(val_re, val_im, conv_re, conv_im, filter_back)
        lag_grad = lax.dynamic_update_slice_in_dim(lag_grad, update, start, 0)
        return (incoming, grad_total, lag_grad)

    def shifted_turn(offset, carry):
        incoming = shifted(carry[0], "seq", -1)
        return turn(offset, (incoming, carry[1], carry[2]))

    lag_zero = jnp.zeros(((cycle_size + 1) * block_rows, channels), jnp.float32)
    carry = turn(0, (grad_conv, empty, lag_zero))
    carry = lax.fori_loop(1, cycle_size, shifted_turn, carry)
    grad_total = carry[1]
    grad_filter = lax.psum_scatter(carry[2][block_rows:], "seq", scatter_dimension=0, tiled=True)
    return (grad_total.astype(jnp.bfloat16), grad_gate, grad_filter, grad_weight)


def packed_tables(rows):
    period = 2 * rows
    freq = np.arange(rows)
    pos = np.arange(period)
    angle = (np.outer(pos, freq) % period) * (2.0 * np.pi / period)
    cosine, sine = np.cos(angle), np.sin(angle)
    alternating = 1.0 - 2.0 * (pos % 2)
    forward_im = -sine
    forward_im[:, 0] = alternating
    forward = np.concatenate([cosine, forward_im], axis=1)
    parity = (1.0 - 2.0 * (freq % 2))[:, None]
    weight = np.where(freq == 0, 1.0, 2.0)[:, None] / period
    back_re = weight * parity * cosine.T
    value_im = weight * parity * sine.T
    lag_im = -value_im
    value_im[0] = alternating / period
    lag_im[0] = alternating / period
    value_back = np.concatenate([back_re, value_im], axis=0)[:, :rows]
    lag_back = np.concatenate([back_re, lag_im], axis=0)
    return tuple(jnp.asarray(t, jnp.bfloat16) for t in (forward, value_back, lag_back))


def mixer_kernel(
    n, nz,
    cot_ref, wt_ref, val_ref, gate_ref, conv_ref, taps_ref, fwd_hbm, vback_hbm, lback_hbm,
    gv_ref, gg_ref, gf_ref, gw_ref,
    val_in, gate_in, conv_in, fwd_ref, vback_ref, lback_ref,
    feat, wall, gated_all, featq, featr, valt, valr, gct, gcr, gvt, gvr, gft, gfr,
    taps, cre, cim, tre, tim, tmix, vre, vim, vmix, sums, lags, pw, pair_out, pair_in, cross_out, cross_in,
    xsem, wzs, wzr, wys, wyr, wcs, wcr, gts, gtr, fts, ftr, vs, vr, cs, cr, os, orr, ls, lr, rs, rr, tsem,
):
    rows = val_in.shape[0]
    group = gct.shape[1]
    bf16, f32 = jnp.bfloat16, jnp.float32
    me = lax.axis_index("seq")
    fs = lax.axis_index("fsdp")
    zi, q = me // 4, me % 4
    y, core = q // 2, q % 2
    quad = [
        (1 - y if k >= 2 else y) * 2 + (1 - core if k % 2 else core) for k in range(4)
    ]
    pair = zi + 1 - 2 * (zi % 2)
    cross = lax.rem(zi + 2, 4)
    far = lax.rem(pair + 2, 4)
    levels = [zi, cross, pair, far]

    def at(level, k):
        return levels[level] * 4 + quad[k]

    def send(src, dst, send_sem, recv_sem, seq, fsdp=None):
        return pltpu.make_async_remote_copy(
            src_ref=src, dst_ref=dst, send_sem=send_sem, recv_sem=recv_sem,
            device_id=(seq, fs if fsdp is None else fsdp), device_id_type=MESH,
        )

    local = [
        pltpu.make_async_copy(src, dst, tsem.at[i]) for i, (src, dst) in enumerate([
            (wt_ref, wall.at[me]),
            (cot_ref, feat.at[fs]),
            (gate_ref, gate_in),
            (conv_ref, conv_in),
            (val_ref, val_in),
            (taps_ref.at[pl.ds(pl.multiple_of(me * group, group), group), :], taps.at[:, rows:]),
            (fwd_hbm, fwd_ref),
            (vback_hbm, vback_ref),
            (lback_hbm, lback_ref),
        ])
    ]
    for copy in local:
        copy.start()

    barrier = pltpu.get_barrier_semaphore()
    for k in range(1, n):
        pl.semaphore_signal(
            barrier, inc=1, device_id=(lax.rem(me + k, n), fs), device_id_type=MESH
        )
    pl.semaphore_signal(barrier, inc=1, device_id=(me, 1 - fs), device_id_type=MESH)
    taps[:, :rows] = jnp.zeros((group, rows), bf16)
    pl.semaphore_wait(barrier, n)

    pending = []

    def go(copy):
        copy.start()
        pending.append(copy)
        return copy

    own = wall.at[me]
    go(send(wt_ref, own, wzs.at[1], wzr.at[1], at(1, 0)))
    go(send(wt_ref, own, wzs.at[2], wzr.at[2], at(2, 0)))
    go(send(wt_ref, own, wys.at[0], wyr.at[0], at(0, 2)))
    x_copy = go(send(cot_ref, feat.at[fs], xsem.at[0], xsem.at[1], me, 1 - fs))
    go(send(wt_ref, own, wcs.at[0], wcr.at[0], at(0, 1)))

    def all_to_all(src, dst, send_sems, recv_sems):
        dst[me] = src[me]
        for k in range(1, n):
            to = lax.rem(me + k, n)
            go(send(src.at[to], dst.at[me], send_sems.at[k], recv_sems.at[k], to))

    def arrive(src, dst, send_sems, recv_sems):
        for k in range(1, n):
            origin = lax.rem(me + n - k, n)
            send(src.at[me], dst.at[origin], send_sems.at[k], recv_sems.at[k], origin).wait_recv()

    for copy in local:
        copy.wait()
    gated_all[q] = (gate_in[...].astype(f32) * conv_in[...].astype(f32)).astype(bf16)
    go(send(gated_all.at[q], gated_all.at[q], gts.at[2], gtr.at[2], at(0, 2)))
    go(send(gated_all.at[q], gated_all.at[q], gts.at[1], gtr.at[1], at(0, 1)))
    valt[...] = val_in[...].astype(f32).T.astype(bf16).reshape(n, group, rows)

    def weight_from(level):
        slot = wall.at[at(level, 0)]
        send(slot, slot, wzs.at[level], wzr.at[level], at(level, 0)).wait_recv()
        if level == 1:
            go(send(slot, slot, wzs.at[3], wzr.at[3], at(2, 0)))
        go(send(slot, slot, wys.at[level], wyr.at[level], at(0, 2)))
        go(send(slot, slot, wcs.at[level], wcr.at[level], at(0, 1)))

    lane = lax.broadcasted_iota(jnp.int32, (n, group, rows), 2)

    def split(spec, re_ref, im_ref, mix_ref, sign):
        real = spec[:, :rows].reshape(n, group, rows)
        imag = spec[:, rows:].reshape(n, group, rows)
        re_ref[...] = real
        if mix_ref is None:
            im_ref[...] = imag
        else:
            im_ref[...] = jnp.where(lane == 0, 0.0, imag)
            mix_ref[...] = jnp.where(lane == 0, sign * imag, real)

    def spectra(source, re_ref, im_ref, mix_ref):
        blocks = source[...].reshape(n * group, rows)
        spec = jnp.dot(blocks, fwd_ref[:rows, :], preferred_element_type=f32)
        split(spec, re_ref, im_ref, mix_ref, 1.0)

    windows = jnp.concatenate(
        [taps[:, m * rows:(m + 2) * rows] for m in range(n)], axis=0
    )
    spec = jnp.dot(windows, fwd_ref[...], preferred_element_type=f32)
    split(spec, tre, tim, tmix, -1.0)

    weight_from(1)
    weight_from(2)
    weight_from(3)
    all_to_all(valt, valr, vs, vr)
    x_copy.wait_recv()
    for part in range(2):
        turned = feat[part].astype(f32).T.astype(bf16)
        per = turned.shape[0] // n * 2
        for j in range(n // 2):
            s = part * (n // 2) + j
            featq[s % 4, s // 4] = turned[j * per:(j + 1) * per]
    featr[q] = featq[q]
    for k in range(1, 4):
        go(send(featq.at[quad[k]], featr.at[q], fts.at[k], ftr.at[k], at(0, k)))

    for level in range(nz):
        slot = wall.at[at(level, 2)]
        send(slot, slot, wys.at[level], wyr.at[level], at(0, 2)).wait_recv()
        go(send(slot, slot, wcs.at[nz + level], wcr.at[nz + level], at(0, 1)))
    far_gated = gated_all.at[quad[2]]
    send(far_gated, far_gated, gts.at[2], gtr.at[2], at(0, 2)).wait_recv()
    go(send(far_gated, far_gated, gts.at[3], gtr.at[3], at(0, 1)))
    for k in range(2 * nz):
        slot = wall.at[at(k % nz, 1 if k < nz else 3)]
        send(slot, slot, wcs.at[k], wcr.at[k], at(0, 1)).wait_recv()

    half = n // 2
    width = wall.shape[2]
    mixed = jnp.dot(
        feat[0], wall[:half].reshape(-1, width), preferred_element_type=f32
    ) + jnp.dot(feat[1], wall[half:].reshape(-1, width), preferred_element_type=f32)
    gct[...] = (mixed * gate_in[...].astype(f32)).T.astype(bf16).reshape(n, group, rows)
    all_to_all(gct, gcr, cs, cr)
    gg_ref[...] = (mixed * conv_in[...].astype(f32)).astype(bf16)

    for k in range(1, 4):
        there = gated_all.at[quad[k]]
        if k != 2:
            send(there, there, gts.at[k], gtr.at[k], at(0, k)).wait_recv()
        send(featq.at[q], featr.at[quad[k]], fts.at[k], ftr.at[k], at(0, k)).wait_recv()

    slices, width = featr.shape[2], gated_all.shape[2]
    tokens = jnp.concatenate(
        [featr[k].reshape(nz * slices, rows) for k in range(4)], axis=1
    )
    pw[...] = jnp.dot(
        tokens, gated_all[...].reshape(4 * rows, width), preferred_element_type=f32
    ).reshape(nz, slices, width)

    pair_out[0] = pw[levels[3]].astype(bf16)
    go(send(pair_out.at[0], pair_in.at[0], rs.at[0], rr.at[0], at(2, 0)))
    pair_out[1] = pw[levels[2]].astype(bf16)
    go(send(pair_out.at[1], pair_in.at[1], rs.at[1], rr.at[1], at(2, 0)))

    arrive(valt, valr, vs, vr)
    spectra(valr, vre, vim, vmix)
    arrive(gct, gcr, cs, cr)
    spectra(gcr, cre, cim, None)

    def value_rows(r, carry):
        at_rows = pl.ds(pl.multiple_of(r * 8, 8), 8)
        for i in range(n):
            c_re, c_im = cre[i:n, at_rows, :], cim[i:n, at_rows, :]
            t_re, t_im = tre[:n - i, at_rows, :], tim[:n - i, at_rows, :]
            t_mix = tmix[:n - i, at_rows, :]
            sums[i, at_rows, :rows] = jnp.sum(c_re * t_re + c_im * t_im, axis=0)
            sums[i, at_rows, rows:] = jnp.sum(c_re * t_im - c_im * t_mix, axis=0)
        return carry

    lax.fori_loop(0, group // 8, value_rows, 0)
    packed = sums[...].astype(bf16).reshape(n * group, 2 * rows)
    blocks = jnp.dot(packed, vback_ref[...], preferred_element_type=f32)
    gvt[...] = blocks.astype(bf16).reshape(n, group, rows)
    all_to_all(gvt, gvr, os, orr)

    send(pair_out.at[0], pair_in.at[0], rs.at[0], rr.at[0], at(2, 0)).wait_recv()
    cross_out[...] = (pw[levels[1]] + pair_in[0].astype(f32)).astype(bf16)
    go(send(cross_out, cross_in, rs.at[2], rr.at[2], at(1, 0)))

    def lag_rows(r, carry):
        at_rows = pl.ds(pl.multiple_of(r * 8, 8), 8)
        for m in range(n):
            c_re, c_im = cre[m:n, at_rows, :], cim[m:n, at_rows, :]
            v_re, v_im = vre[:n - m, at_rows, :], vim[:n - m, at_rows, :]
            v_mix = vmix[:n - m, at_rows, :]
            lags[m, at_rows, :rows] = jnp.sum(v_re * c_re + v_im * c_im, axis=0)
            lags[m, at_rows, rows:] = jnp.sum(v_mix * c_im - v_im * c_re, axis=0)
        return carry

    lax.fori_loop(0, group // 8, lag_rows, 0)
    packed = lags[...].astype(bf16).reshape(n * group, 2 * rows)
    parts = jnp.dot(packed, lback_ref[...], preferred_element_type=f32)
    first = jnp.concatenate([parts[group:, :rows], jnp.zeros((group, rows), f32)], axis=0)
    gft[...] = (parts[:, rows:] + first).astype(bf16).reshape(n, group, rows)
    all_to_all(gft, gfr, ls, lr)

    send(pair_out.at[1], pair_in.at[1], rs.at[1], rr.at[1], at(2, 0)).wait_recv()
    send(cross_out, cross_in, rs.at[2], rr.at[2], at(1, 0)).wait_recv()
    gw_ref[...] = pw[zi] + pair_in[1].astype(f32) + cross_in[...].astype(f32)
    arrive(gvt, gvr, os, orr)
    gv_ref[...] = gvr[...].reshape(n * group, rows)
    arrive(gft, gfr, ls, lr)
    gf_ref[...] = gfr[...].reshape(n * group, rows)
    for copy in pending:
        copy.wait_send()


def finish_kernel(gv_ref, gg_ref, gf_ref, gw_ref, gv_out, gg_out, gf_out, gw_out):
    gv_out[...] = gv_ref[...].astype(jnp.float32).T.astype(jnp.bfloat16)
    gg_out[...] = gg_ref[...]
    gf_out[...] = gf_ref[...].astype(jnp.float32).T
    gw_out[...] = gw_ref[...]


def split_body(cotangent, out_weight, values, gate_input, conv_out, filter_taps):
    rows, channels = values.shape
    n = lax.axis_size("seq")
    nz = n // 4
    group = channels // n
    slice_cols = out_weight.shape[1]
    forward, value_back, lag_back = packed_tables(rows)
    bf16, f32 = jnp.bfloat16, jnp.float32
    vm = pltpu.VMEM
    dma = pltpu.SemaphoreType.DMA
    trip = (n, group, rows)
    vmem = pl.BlockSpec(memory_space=pltpu.VMEM)
    gv, gg, gf, gw = pl.pallas_call(
        functools.partial(mixer_kernel, n, nz),
        out_shape=(
            jax.ShapeDtypeStruct((channels, rows), bf16),
            jax.ShapeDtypeStruct((rows, channels), bf16),
            jax.ShapeDtypeStruct((channels, rows), bf16),
            jax.ShapeDtypeStruct((slice_cols, channels), f32),
        ),
        in_specs=[pl.BlockSpec(memory_space=pltpu.HBM)] * 9,
        out_specs=(vmem,) * 4,
        scratch_shapes=[vm((rows, channels), bf16)] * 3 + [
            vm((2 * rows, 2 * rows), bf16),
            vm((2 * rows, rows), bf16),
            vm((2 * rows, 2 * rows), bf16),
            vm((2, rows, channels), bf16),
            vm((n, slice_cols, channels), bf16),
            vm((4, rows, channels), bf16),
            vm((4, nz, slice_cols, rows), bf16),
            vm((4, nz, slice_cols, rows), bf16),
        ] + [vm(trip, bf16)] * 8 + [
            vm((group, (n + 1) * rows), bf16),
        ] + [vm(trip, f32)] * 8 + [
            vm((n, group, 2 * rows), f32),
            vm((n, group, 2 * rows), f32),
            vm((nz, slice_cols, channels), f32),
            vm((2, slice_cols, channels), bf16),
            vm((2, slice_cols, channels), bf16),
            vm((slice_cols, channels), bf16),
            vm((slice_cols, channels), bf16),
            dma((2,)),
            dma((nz,)), dma((nz,)), dma((nz,)), dma((nz,)), dma((2 * nz,)), dma((2 * nz,)),
            dma((4,)), dma((4,)), dma((4,)), dma((4,)),
        ] + [dma((n,))] * 8 + [dma((3,)), dma((3,)), dma((9,))],
        compiler_params=pltpu.CompilerParams(
            collective_id=0, has_side_effects=True, vmem_limit_bytes=60 * 1024 * 1024
        ),
    )(
        cotangent, out_weight.T, values, gate_input, conv_out, filter_taps,
        forward, value_back, lag_back,
    )
    gv, gg, gf, gw = pl.pallas_call(
        finish_kernel,
        out_shape=(
            jax.ShapeDtypeStruct((rows, channels), bf16),
            jax.ShapeDtypeStruct((rows, channels), bf16),
            jax.ShapeDtypeStruct((rows, channels), f32),
            jax.ShapeDtypeStruct((slice_cols, channels), f32),
        ),
        in_specs=[vmem] * 4,
        out_specs=(vmem,) * 4,
        compiler_params=pltpu.CompilerParams(vmem_limit_bytes=60 * 1024 * 1024),
    )(gv, gg, gf, gw)
    return gv, gg, gf, gw.T


def solution(mesh):
    in_specs = (
        P("seq", "fsdp"),
        P("fsdp", "seq"),
        P("seq", "fsdp"),
        P("seq", "fsdp"),
        P("seq", "fsdp"),
        P("fsdp", None),
    )
    out_specs = (P("seq", "fsdp"), P("seq", "fsdp"), P("seq", "fsdp"), P("fsdp", "seq"))

    def body(*blocks):
        rows, channels = blocks[2].shape
        n = mesh.shape["seq"]
        aligned = rows % 128 == 0 and channels % (16 * n) == 0 and blocks[1].shape[1] % 16 == 0
        if aligned and n == 16 and mesh.shape["fsdp"] == 2:
            return split_body(*blocks)
        return ring_body(*blocks)

    return jax.shard_map(body, mesh=mesh, in_specs=in_specs, out_specs=out_specs, check_vma=False)
```

```python
import functools

import jax
import jax.numpy as jnp
import numpy as np
from jax import lax
from jax.experimental import pallas as pl
from jax.experimental.pallas import tpu as pltpu
from jax.sharding import PartitionSpec as P

MESH = pl.DeviceIdType.MESH


def shifted(block, axis, distance):
    devices = range(lax.axis_size(axis))
    route = [(i - distance, i) for i in devices if i - distance in devices]
    return lax.ppermute(block, axis, route)


def make_tables(block_rows):
    period = 2 * block_rows
    frequency = lax.broadcasted_iota(jnp.int32, (period, period), 0)
    position = lax.broadcasted_iota(jnp.int32, (period, period), 1)
    angles = (frequency * position % period).astype(jnp.float32) * (2.0 * jnp.pi / period)
    cosine = jnp.cos(angles)
    sine_part = jnp.sin(angles)
    parity = 1.0 - 2.0 * (position % 2).astype(jnp.float32)
    dft_cos = cosine.astype(jnp.bfloat16)
    dft_sin = (-sine_part).astype(jnp.bfloat16)
    back_cos = (parity * cosine / period).astype(jnp.bfloat16)
    back_sin = (-parity * sine_part / period).astype(jnp.bfloat16)
    return (dft_cos, dft_sin, back_cos, back_sin)


def narrow_dot(left, right):
    return jnp.dot(left, right, preferred_element_type=jnp.float32)


def product_rows(table, window):
    return lax.dot_general(
        table, window, (((1,), (1,)), ((), ())), preferred_element_type=jnp.float32
    )


def spectrum(block, cos_part, sin_part):
    return (narrow_dot(cos_part, block), narrow_dot(sin_part, block))


def value_term(conv_re, conv_im, filt_re, filt_im, back_table):
    mixed_re = conv_re * filt_re + conv_im * filt_im
    mixed_im = conv_re * filt_im - conv_im * filt_re
    stacked = jnp.concatenate(
        [mixed_re.astype(jnp.bfloat16), mixed_im.astype(jnp.bfloat16)], axis=0
    )
    return narrow_dot(back_table, stacked)


def filter_term(val_re, val_im, conv_re, conv_im, back_table):
    mixed_re = val_re * conv_re + val_im * conv_im
    mixed_im = val_re * conv_im - val_im * conv_re
    stacked = jnp.concatenate(
        [mixed_re.astype(jnp.bfloat16), mixed_im.astype(jnp.bfloat16)], axis=0
    )
    return narrow_dot(back_table, stacked)


def ring_body(cotangent, out_weight, values, gate_input, conv_out, filter_taps):
    block_rows, channels = values.shape
    cycle_size = lax.axis_size("seq")
    weight_rows = lax.all_gather(out_weight, "seq", axis=1, tiled=True)
    features = lax.all_gather(cotangent, "fsdp", axis=1, tiled=True)
    grad_mixed = lax.dot_general(
        features, weight_rows, (((1,), (1,)), ((), ())), preferred_element_type=jnp.float32
    )
    gate_wide = gate_input.astype(jnp.float32)
    conv_wide = conv_out.astype(jnp.float32)
    grad_gate = (grad_mixed * conv_wide).astype(jnp.bfloat16)
    grad_conv = (grad_mixed * gate_wide).astype(jnp.bfloat16)
    gated = (gate_wide * conv_wide).astype(jnp.bfloat16)
    weight_terms = lax.dot_general(
        gated, features, (((0,), (0,)), ((), ())), preferred_element_type=jnp.float32
    )
    grad_weight = lax.psum_scatter(weight_terms, "seq", scatter_dimension=1, tiled=True)
    period = 2 * block_rows
    dft_cos, dft_sin, back_cos, back_sin = make_tables(block_rows)
    block_cos = dft_cos[:, :block_rows]
    block_sin = dft_sin[:, :block_rows]
    value_back = jnp.concatenate([back_cos[:block_rows], -back_sin[:block_rows]], axis=1)
    filter_back = jnp.concatenate([back_cos, back_sin], axis=1)
    padded_taps = jnp.concatenate(
        [jnp.zeros((channels, block_rows), jnp.bfloat16), filter_taps], axis=1
    )
    empty = jnp.zeros((block_rows, channels), jnp.float32)

    def window_spectrum(offset):
        window = lax.dynamic_slice_in_dim(padded_taps, offset * block_rows, period, 1)
        return (product_rows(dft_cos, window), product_rows(dft_sin, window))

    val_re, val_im = spectrum(values, block_cos, block_sin)

    def turn(offset, carry):
        incoming, grad_total, lag_grad = carry
        conv_re, conv_im = spectrum(incoming, block_cos, block_sin)
        filt_re, filt_im = window_spectrum(offset)
        grad_total = grad_total + value_term(conv_re, conv_im, filt_re, filt_im, value_back)
        start = offset * block_rows
        current = lax.dynamic_slice_in_dim(lag_grad, start, period, 0)
        update = current + filter_term(val_re, val_im, conv_re, conv_im, filter_back)
        lag_grad = lax.dynamic_update_slice_in_dim(lag_grad, update, start, 0)
        return (incoming, grad_total, lag_grad)

    def shifted_turn(offset, carry):
        incoming = shifted(carry[0], "seq", -1)
        return turn(offset, (incoming, carry[1], carry[2]))

    lag_zero = jnp.zeros(((cycle_size + 1) * block_rows, channels), jnp.float32)
    carry = turn(0, (grad_conv, empty, lag_zero))
    carry = lax.fori_loop(1, cycle_size, shifted_turn, carry)
    grad_total = carry[1]
    grad_filter = lax.psum_scatter(carry[2][block_rows:], "seq", scatter_dimension=0, tiled=True)
    return (grad_total.astype(jnp.bfloat16), grad_gate, grad_filter, grad_weight)


def packed_tables(rows):
    period = 2 * rows
    freq = np.arange(rows)
    pos = np.arange(period)
    angle = (np.outer(pos, freq) % period) * (2.0 * np.pi / period)
    cosine, sine = np.cos(angle), np.sin(angle)
    alternating = 1.0 - 2.0 * (pos % 2)
    forward_im = -sine
    forward_im[:, 0] = alternating
    forward = np.concatenate([cosine, forward_im], axis=1)
    parity = (1.0 - 2.0 * (freq % 2))[:, None]
    weight = np.where(freq == 0, 1.0, 2.0)[:, None] / period
    back_re = weight * parity * cosine.T
    value_im = weight * parity * sine.T
    lag_im = -value_im
    value_im[0] = alternating / period
    lag_im[0] = alternating / period
    value_back = np.concatenate([back_re, value_im], axis=0)[:, :rows]
    lag_back = np.concatenate([back_re, lag_im], axis=0)
    return tuple(jnp.asarray(t, jnp.bfloat16) for t in (forward, value_back, lag_back))


def mixer_kernel(
    n, nz,
    cot_ref, wt_ref, val_ref, gate_ref, conv_ref, taps_ref, fwd_hbm, vback_hbm, lback_hbm,
    gv_ref, gg_ref, gf_ref, gw_ref,
    val_in, gate_in, conv_in, fwd_ref, vback_ref, lback_ref,
    feat, wall, gated_all, featq, featr, valt, valr, gct, gcr, gvt, gvr, gft, gfr,
    taps, cre, cim, tre, tim, tmix, vre, vim, vmix, sums, lags, pw, pair_out, pair_in, cross_out, cross_in,
    shares, core_in, y_out, y_in,
    xsem, wzs, wzr, ms, mr, gts, gtr, fts, ftr, vs, vr, cs, cr, os, orr, ls, lr, rs, rr, tsem,
):
    rows = val_in.shape[0]
    group = gct.shape[1]
    bf16, f32 = jnp.bfloat16, jnp.float32
    me = lax.axis_index("seq")
    fs = lax.axis_index("fsdp")
    zi, q = me // 4, me % 4
    y, core = q // 2, q % 2
    quad = [
        (1 - y if k >= 2 else y) * 2 + (1 - core if k % 2 else core) for k in range(4)
    ]
    pair = zi + 1 - 2 * (zi % 2)
    cross = lax.rem(zi + 2, 4)
    far = lax.rem(pair + 2, 4)
    levels = [zi, cross, pair, far]

    def at(level, k):
        return levels[level] * 4 + quad[k]

    def send(src, dst, send_sem, recv_sem, seq, fsdp=None):
        return pltpu.make_async_remote_copy(
            src_ref=src, dst_ref=dst, send_sem=send_sem, recv_sem=recv_sem,
            device_id=(seq, fs if fsdp is None else fsdp), device_id_type=MESH,
        )

    local = [
        pltpu.make_async_copy(src, dst, tsem.at[i]) for i, (src, dst) in enumerate([
            (wt_ref, wall.at[zi]),
            (cot_ref, feat.at[fs]),
            (gate_ref, gate_in),
            (conv_ref, conv_in),
            (val_ref, val_in),
            (taps_ref.at[pl.ds(pl.multiple_of(me * group, group), group), :], taps.at[:, rows:]),
            (fwd_hbm, fwd_ref),
            (vback_hbm, vback_ref),
            (lback_hbm, lback_ref),
        ])
    ]
    for copy in local:
        copy.start()

    barrier = pltpu.get_barrier_semaphore()
    for k in range(1, n):
        pl.semaphore_signal(
            barrier, inc=1, device_id=(lax.rem(me + k, n), fs), device_id_type=MESH
        )
    pl.semaphore_signal(barrier, inc=1, device_id=(me, 1 - fs), device_id_type=MESH)
    taps[:, :rows] = jnp.zeros((group, rows), bf16)
    pl.semaphore_wait(barrier, n)

    pending = []

    def go(copy):
        copy.start()
        pending.append(copy)
        return copy

    own = wall.at[zi]
    x_copy = go(send(cot_ref, feat.at[fs], xsem.at[0], xsem.at[1], me, 1 - fs))
    go(send(wt_ref, own, wzs.at[1], wzr.at[1], at(1, 0)))
    go(send(wt_ref, own, wzs.at[2], wzr.at[2], at(2, 0)))

    def all_to_all(src, dst, send_sems, recv_sems):
        dst[me] = src[me]
        for k in range(1, n):
            to = lax.rem(me + k, n)
            go(send(src.at[to], dst.at[me], send_sems.at[k], recv_sems.at[k], to))

    def arrive(src, dst, send_sems, recv_sems):
        for k in range(1, n):
            origin = lax.rem(me + n - k, n)
            send(src.at[me], dst.at[origin], send_sems.at[k], recv_sems.at[k], origin).wait_recv()

    for copy in local:
        copy.wait()
    gated_all[q] = (gate_in[...].astype(f32) * conv_in[...].astype(f32)).astype(bf16)
    go(send(gated_all.at[q], gated_all.at[q], gts.at[2], gtr.at[2], at(0, 2)))
    go(send(gated_all.at[q], gated_all.at[q], gts.at[1], gtr.at[1], at(0, 1)))
    valt[...] = val_in[...].astype(f32).T.astype(bf16).reshape(n, group, rows)

    def weight_from(level):
        slot = wall.at[levels[level]]
        send(slot, slot, wzs.at[level], wzr.at[level], at(level, 0)).wait_recv()
        if level == 1:
            go(send(slot, slot, wzs.at[3], wzr.at[3], at(2, 0)))

    lane = lax.broadcasted_iota(jnp.int32, (n, group, rows), 2)

    def split(spec, re_ref, im_ref, mix_ref, sign):
        real = spec[:, :rows].reshape(n, group, rows)
        imag = spec[:, rows:].reshape(n, group, rows)
        re_ref[...] = real
        if mix_ref is None:
            im_ref[...] = imag
        else:
            im_ref[...] = jnp.where(lane == 0, 0.0, imag)
            mix_ref[...] = jnp.where(lane == 0, sign * imag, real)

    def spectra(source, re_ref, im_ref, mix_ref):
        blocks = source[...].reshape(n * group, rows)
        spec = jnp.dot(blocks, fwd_ref[:rows, :], preferred_element_type=f32)
        split(spec, re_ref, im_ref, mix_ref, 1.0)

    x_copy.wait_recv()
    for part in range(2):
        turned = feat[part].astype(f32).T.astype(bf16)
        per = turned.shape[0] // n * 2
        for j in range(n // 2):
            s = part * (n // 2) + j
            featq[s % 4, s // 4] = turned[j * per:(j + 1) * per]
    featr[q] = featq[q]
    for k in (2, 3, 1):
        go(send(featq.at[quad[k]], featr.at[q], fts.at[k], ftr.at[k], at(0, k)))
    weight_from(1)

    windows = jnp.concatenate(
        [taps[:, m * rows:(m + 2) * rows] for m in range(n)], axis=0
    )
    spec = jnp.dot(windows, fwd_ref[...], preferred_element_type=f32)
    split(spec, tre, tim, tmix, -1.0)

    for k in range(1, 4):
        send(featq.at[q], featr.at[quad[k]], fts.at[k], ftr.at[k], at(0, k)).wait_recv()
    slices, width = featr.shape[2], gated_all.shape[2]
    tokens = jnp.concatenate(
        [featr[k].reshape(nz * slices, rows) for k in range(4)], axis=1
    )
    weight_from(2)
    weight_from(3)
    partial = jnp.dot(
        tokens.astype(f32).T.astype(bf16),
        wall[...].reshape(nz * slices, width),
        preferred_element_type=f32,
    )
    for k in range(4):
        shares[k % 2, k // 2] = partial[k * rows:(k + 1) * rows]
    core_copy = go(send(shares.at[1 - core], core_in, ms.at[0], mr.at[0], at(0, 1)))

    far_gated = gated_all.at[quad[2]]
    send(far_gated, far_gated, gts.at[2], gtr.at[2], at(0, 2)).wait_recv()
    go(send(far_gated, far_gated, gts.at[3], gtr.at[3], at(0, 1)))

    core_copy.wait_recv()
    y_out[...] = (shares[core, 1 - y] + core_in[1 - y]).astype(bf16)
    y_copy = go(send(y_out, y_in, ms.at[1], mr.at[1], at(0, 2)))

    for k in (1, 3):
        there = gated_all.at[quad[k]]
        send(there, there, gts.at[k], gtr.at[k], at(0, k)).wait_recv()
    pw[...] = jnp.dot(
        tokens, gated_all[...].reshape(4 * rows, width), preferred_element_type=f32
    ).reshape(nz, slices, width)

    pair_out[0] = pw[levels[3]].astype(bf16)
    go(send(pair_out.at[0], pair_in.at[0], rs.at[0], rr.at[0], at(2, 0)))
    pair_out[1] = pw[levels[2]].astype(bf16)
    go(send(pair_out.at[1], pair_in.at[1], rs.at[1], rr.at[1], at(2, 0)))

    y_copy.wait_recv()
    mixed = shares[core, y] + core_in[y] + y_in[...].astype(f32)
    gct[...] = (mixed * gate_in[...].astype(f32)).T.astype(bf16).reshape(n, group, rows)
    all_to_all(gct, gcr, cs, cr)
    gg_ref[...] = (mixed * conv_in[...].astype(f32)).astype(bf16)
    all_to_all(valt, valr, vs, vr)

    arrive(gct, gcr, cs, cr)
    spectra(gcr, cre, cim, None)
    send(pair_out.at[0], pair_in.at[0], rs.at[0], rr.at[0], at(2, 0)).wait_recv()
    cross_out[...] = (pw[levels[1]] + pair_in[0].astype(f32)).astype(bf16)
    go(send(cross_out, cross_in, rs.at[2], rr.at[2], at(1, 0)))

    def value_rows(r, carry):
        at_rows = pl.ds(pl.multiple_of(r * 8, 8), 8)
        for i in range(n):
            c_re, c_im = cre[i:n, at_rows, :], cim[i:n, at_rows, :]
            t_re, t_im = tre[:n - i, at_rows, :], tim[:n - i, at_rows, :]
            t_mix = tmix[:n - i, at_rows, :]
            sums[i, at_rows, :rows] = jnp.sum(c_re * t_re + c_im * t_im, axis=0)
            sums[i, at_rows, rows:] = jnp.sum(c_re * t_im - c_im * t_mix, axis=0)
        return carry

    lax.fori_loop(0, group // 8, value_rows, 0)
    packed = sums[...].astype(bf16).reshape(n * group, 2 * rows)
    blocks = jnp.dot(packed, vback_ref[...], preferred_element_type=f32)
    gvt[...] = blocks.astype(bf16).reshape(n, group, rows)
    all_to_all(gvt, gvr, os, orr)

    arrive(valt, valr, vs, vr)
    spectra(valr, vre, vim, vmix)

    def lag_rows(r, carry):
        at_rows = pl.ds(pl.multiple_of(r * 8, 8), 8)
        for m in range(n):
            c_re, c_im = cre[m:n, at_rows, :], cim[m:n, at_rows, :]
            v_re, v_im = vre[:n - m, at_rows, :], vim[:n - m, at_rows, :]
            v_mix = vmix[:n - m, at_rows, :]
            lags[m, at_rows, :rows] = jnp.sum(v_re * c_re + v_im * c_im, axis=0)
            lags[m, at_rows, rows:] = jnp.sum(v_mix * c_im - v_im * c_re, axis=0)
        return carry

    lax.fori_loop(0, group // 8, lag_rows, 0)
    packed = lags[...].astype(bf16).reshape(n * group, 2 * rows)
    parts = jnp.dot(packed, lback_ref[...], preferred_element_type=f32)
    first = jnp.concatenate([parts[group:, :rows], jnp.zeros((group, rows), f32)], axis=0)
    gft[...] = (parts[:, rows:] + first).astype(bf16).reshape(n, group, rows)
    all_to_all(gft, gfr, ls, lr)

    send(pair_out.at[1], pair_in.at[1], rs.at[1], rr.at[1], at(2, 0)).wait_recv()
    send(cross_out, cross_in, rs.at[2], rr.at[2], at(1, 0)).wait_recv()
    gw_ref[...] = pw[zi] + pair_in[1].astype(f32) + cross_in[...].astype(f32)
    arrive(gvt, gvr, os, orr)
    gv_ref[...] = gvr[...].reshape(n * group, rows)
    arrive(gft, gfr, ls, lr)
    gf_ref[...] = gfr[...].reshape(n * group, rows)
    for copy in pending:
        copy.wait_send()


def finish_kernel(gv_ref, gg_ref, gf_ref, gw_ref, gv_out, gg_out, gf_out, gw_out):
    gv_out[...] = gv_ref[...].astype(jnp.float32).T.astype(jnp.bfloat16)
    gg_out[...] = gg_ref[...]
    gf_out[...] = gf_ref[...].astype(jnp.float32).T
    gw_out[...] = gw_ref[...]


def split_body(cotangent, out_weight, values, gate_input, conv_out, filter_taps):
    rows, channels = values.shape
    n = lax.axis_size("seq")
    nz = n // 4
    group = channels // n
    slice_cols = out_weight.shape[1]
    forward, value_back, lag_back = packed_tables(rows)
    bf16, f32 = jnp.bfloat16, jnp.float32
    vm = pltpu.VMEM
    dma = pltpu.SemaphoreType.DMA
    trip = (n, group, rows)
    vmem = pl.BlockSpec(memory_space=pltpu.VMEM)
    gv, gg, gf, gw = pl.pallas_call(
        functools.partial(mixer_kernel, n, nz),
        out_shape=(
            jax.ShapeDtypeStruct((channels, rows), bf16),
            jax.ShapeDtypeStruct((rows, channels), bf16),
            jax.ShapeDtypeStruct((channels, rows), bf16),
            jax.ShapeDtypeStruct((slice_cols, channels), f32),
        ),
        in_specs=[pl.BlockSpec(memory_space=pltpu.HBM)] * 9,
        out_specs=(vmem,) * 4,
        scratch_shapes=[vm((rows, channels), bf16)] * 3 + [
            vm((2 * rows, 2 * rows), bf16),
            vm((2 * rows, rows), bf16),
            vm((2 * rows, 2 * rows), bf16),
            vm((2, rows, channels), bf16),
            vm((nz, slice_cols, channels), bf16),
            vm((4, rows, channels), bf16),
            vm((4, nz, slice_cols, rows), bf16),
            vm((4, nz, slice_cols, rows), bf16),
        ] + [vm(trip, bf16)] * 8 + [
            vm((group, (n + 1) * rows), bf16),
        ] + [vm(trip, f32)] * 8 + [
            vm((n, group, 2 * rows), f32),
            vm((n, group, 2 * rows), f32),
            vm((nz, slice_cols, channels), f32),
            vm((2, slice_cols, channels), bf16),
            vm((2, slice_cols, channels), bf16),
            vm((slice_cols, channels), bf16),
            vm((slice_cols, channels), bf16),
            vm((2, 2, rows, channels), f32),
            vm((2, rows, channels), f32),
            vm((rows, channels), bf16),
            vm((rows, channels), bf16),
            dma((2,)),
            dma((nz,)), dma((nz,)), dma((2,)), dma((2,)),
            dma((4,)), dma((4,)), dma((4,)), dma((4,)),
        ] + [dma((n,))] * 8 + [dma((3,)), dma((3,)), dma((9,))],
        compiler_params=pltpu.CompilerParams(
            collective_id=0, has_side_effects=True, vmem_limit_bytes=60 * 1024 * 1024
        ),
    )(
        cotangent, out_weight.T, values, gate_input, conv_out, filter_taps,
        forward, value_back, lag_back,
    )
    gv, gg, gf, gw = pl.pallas_call(
        finish_kernel,
        out_shape=(
            jax.ShapeDtypeStruct((rows, channels), bf16),
            jax.ShapeDtypeStruct((rows, channels), bf16),
            jax.ShapeDtypeStruct((rows, channels), f32),
            jax.ShapeDtypeStruct((slice_cols, channels), f32),
        ),
        in_specs=[vmem] * 4,
        out_specs=(vmem,) * 4,
        compiler_params=pltpu.CompilerParams(vmem_limit_bytes=60 * 1024 * 1024),
    )(gv, gg, gf, gw)
    return gv, gg, gf, gw.T


def solution(mesh):
    in_specs = (
        P("seq", "fsdp"),
        P("fsdp", "seq"),
        P("seq", "fsdp"),
        P("seq", "fsdp"),
        P("seq", "fsdp"),
        P("fsdp", None),
    )
    out_specs = (P("seq", "fsdp"), P("seq", "fsdp"), P("seq", "fsdp"), P("fsdp", "seq"))

    def body(*blocks):
        rows, channels = blocks[2].shape
        n = mesh.shape["seq"]
        aligned = rows % 128 == 0 and channels % (16 * n) == 0 and blocks[1].shape[1] % 16 == 0
        if aligned and n == 16 and mesh.shape["fsdp"] == 2:
            return split_body(*blocks)
        return ring_body(*blocks)

    return jax.shard_map(body, mesh=mesh, in_specs=in_specs, out_specs=out_specs, check_vma=False)
```

```python
import functools

import jax
import jax.numpy as jnp
import numpy as np
from jax import lax
from jax.experimental import pallas as pl
from jax.experimental.pallas import tpu as pltpu
from jax.sharding import PartitionSpec as P

MESH = pl.DeviceIdType.MESH


def shifted(block, axis, distance):
    devices = range(lax.axis_size(axis))
    route = [(i - distance, i) for i in devices if i - distance in devices]
    return lax.ppermute(block, axis, route)


def make_tables(block_rows):
    period = 2 * block_rows
    frequency = lax.broadcasted_iota(jnp.int32, (period, period), 0)
    position = lax.broadcasted_iota(jnp.int32, (period, period), 1)
    angles = (frequency * position % period).astype(jnp.float32) * (2.0 * jnp.pi / period)
    cosine = jnp.cos(angles)
    sine_part = jnp.sin(angles)
    parity = 1.0 - 2.0 * (position % 2).astype(jnp.float32)
    dft_cos = cosine.astype(jnp.bfloat16)
    dft_sin = (-sine_part).astype(jnp.bfloat16)
    back_cos = (parity * cosine / period).astype(jnp.bfloat16)
    back_sin = (-parity * sine_part / period).astype(jnp.bfloat16)
    return (dft_cos, dft_sin, back_cos, back_sin)


def narrow_dot(left, right):
    return jnp.dot(left, right, preferred_element_type=jnp.float32)


def product_rows(table, window):
    return lax.dot_general(
        table, window, (((1,), (1,)), ((), ())), preferred_element_type=jnp.float32
    )


def spectrum(block, cos_part, sin_part):
    return (narrow_dot(cos_part, block), narrow_dot(sin_part, block))


def value_term(conv_re, conv_im, filt_re, filt_im, back_table):
    mixed_re = conv_re * filt_re + conv_im * filt_im
    mixed_im = conv_re * filt_im - conv_im * filt_re
    stacked = jnp.concatenate(
        [mixed_re.astype(jnp.bfloat16), mixed_im.astype(jnp.bfloat16)], axis=0
    )
    return narrow_dot(back_table, stacked)


def filter_term(val_re, val_im, conv_re, conv_im, back_table):
    mixed_re = val_re * conv_re + val_im * conv_im
    mixed_im = val_re * conv_im - val_im * conv_re
    stacked = jnp.concatenate(
        [mixed_re.astype(jnp.bfloat16), mixed_im.astype(jnp.bfloat16)], axis=0
    )
    return narrow_dot(back_table, stacked)


def ring_body(cotangent, out_weight, values, gate_input, conv_out, filter_taps):
    block_rows, channels = values.shape
    cycle_size = lax.axis_size("seq")
    weight_rows = lax.all_gather(out_weight, "seq", axis=1, tiled=True)
    features = lax.all_gather(cotangent, "fsdp", axis=1, tiled=True)
    grad_mixed = lax.dot_general(
        features, weight_rows, (((1,), (1,)), ((), ())), preferred_element_type=jnp.float32
    )
    gate_wide = gate_input.astype(jnp.float32)
    conv_wide = conv_out.astype(jnp.float32)
    grad_gate = (grad_mixed * conv_wide).astype(jnp.bfloat16)
    grad_conv = (grad_mixed * gate_wide).astype(jnp.bfloat16)
    gated = (gate_wide * conv_wide).astype(jnp.bfloat16)
    weight_terms = lax.dot_general(
        gated, features, (((0,), (0,)), ((), ())), preferred_element_type=jnp.float32
    )
    grad_weight = lax.psum_scatter(weight_terms, "seq", scatter_dimension=1, tiled=True)
    period = 2 * block_rows
    dft_cos, dft_sin, back_cos, back_sin = make_tables(block_rows)
    block_cos = dft_cos[:, :block_rows]
    block_sin = dft_sin[:, :block_rows]
    value_back = jnp.concatenate([back_cos[:block_rows], -back_sin[:block_rows]], axis=1)
    filter_back = jnp.concatenate([back_cos, back_sin], axis=1)
    padded_taps = jnp.concatenate(
        [jnp.zeros((channels, block_rows), jnp.bfloat16), filter_taps], axis=1
    )
    empty = jnp.zeros((block_rows, channels), jnp.float32)

    def window_spectrum(offset):
        window = lax.dynamic_slice_in_dim(padded_taps, offset * block_rows, period, 1)
        return (product_rows(dft_cos, window), product_rows(dft_sin, window))

    val_re, val_im = spectrum(values, block_cos, block_sin)

    def turn(offset, carry):
        incoming, grad_total, lag_grad = carry
        conv_re, conv_im = spectrum(incoming, block_cos, block_sin)
        filt_re, filt_im = window_spectrum(offset)
        grad_total = grad_total + value_term(conv_re, conv_im, filt_re, filt_im, value_back)
        start = offset * block_rows
        current = lax.dynamic_slice_in_dim(lag_grad, start, period, 0)
        update = current + filter_term(val_re, val_im, conv_re, conv_im, filter_back)
        lag_grad = lax.dynamic_update_slice_in_dim(lag_grad, update, start, 0)
        return (incoming, grad_total, lag_grad)

    def shifted_turn(offset, carry):
        incoming = shifted(carry[0], "seq", -1)
        return turn(offset, (incoming, carry[1], carry[2]))

    lag_zero = jnp.zeros(((cycle_size + 1) * block_rows, channels), jnp.float32)
    carry = turn(0, (grad_conv, empty, lag_zero))
    carry = lax.fori_loop(1, cycle_size, shifted_turn, carry)
    grad_total = carry[1]
    grad_filter = lax.psum_scatter(carry[2][block_rows:], "seq", scatter_dimension=0, tiled=True)
    return (grad_total.astype(jnp.bfloat16), grad_gate, grad_filter, grad_weight)


def packed_tables(rows):
    period = 2 * rows
    freq = np.arange(rows)
    pos = np.arange(period)
    angle = (np.outer(pos, freq) % period) * (2.0 * np.pi / period)
    cosine, sine = np.cos(angle), np.sin(angle)
    alternating = 1.0 - 2.0 * (pos % 2)
    forward_im = -sine
    forward_im[:, 0] = alternating
    forward = np.concatenate([cosine, forward_im], axis=1)
    parity = (1.0 - 2.0 * (freq % 2))[:, None]
    weight = np.where(freq == 0, 1.0, 2.0)[:, None] / period
    back_re = weight * parity * cosine.T
    value_im = weight * parity * sine.T
    lag_im = -value_im
    value_im[0] = alternating / period
    lag_im[0] = alternating / period
    value_back = np.concatenate([back_re, value_im], axis=0)[:, :rows]
    lag_back = np.concatenate([back_re, lag_im], axis=0)
    return tuple(jnp.asarray(t, jnp.bfloat16) for t in (forward, value_back, lag_back))


def mixer_kernel(
    n, nz,
    cot_ref, wt_ref, val_ref, gate_ref, conv_ref, taps_ref, fwd_hbm, vback_hbm, lback_hbm,
    gv_ref, gg_ref, gf_ref, gw_ref,
    val_in, gate_in, conv_in, fwd_ref, vback_ref, lback_ref,
    feat, wall, gated_all, featq, featr, valt, valr, gct, gcr, gvt, gvr, gft, gfr,
    taps, cre, cim, tre, tim, tmix, vre, vim, vmix, sums, lags, pw, pair_out, pair_in, cross_out, cross_in,
    shares, core_in, y_out, y_in,
    xsem, wzs, wzr, ms, mr, gts, gtr, fts, ftr, vs, cs, os, ls, rs, rr, tsem,
):
    rows = val_in.shape[0]
    group = gct.shape[1]
    bf16, f32 = jnp.bfloat16, jnp.float32
    me = lax.axis_index("seq")
    fs = lax.axis_index("fsdp")
    zi, q = me // 4, me % 4
    y, core = q // 2, q % 2
    quad = [
        (1 - y if k >= 2 else y) * 2 + (1 - core if k % 2 else core) for k in range(4)
    ]
    pair = zi + 1 - 2 * (zi % 2)
    cross = lax.rem(zi + 2, 4)
    far = lax.rem(pair + 2, 4)
    levels = [zi, cross, pair, far]

    def at(level, k):
        return levels[level] * 4 + quad[k]

    def send(src, dst, send_sem, recv_sem, seq, fsdp=None):
        return pltpu.make_async_remote_copy(
            src_ref=src, dst_ref=dst, send_sem=send_sem, recv_sem=recv_sem,
            device_id=(seq, fs if fsdp is None else fsdp), device_id_type=MESH,
        )

    local = [
        pltpu.make_async_copy(src, dst, tsem.at[i]) for i, (src, dst) in enumerate([
            (wt_ref, wall.at[zi]),
            (cot_ref, feat.at[fs]),
            (gate_ref, gate_in),
            (conv_ref, conv_in),
            (val_ref, val_in),
            (taps_ref.at[pl.ds(pl.multiple_of(me * group, group), group), :], taps.at[:, rows:]),
            (fwd_hbm, fwd_ref),
            (vback_hbm, vback_ref),
            (lback_hbm, lback_ref),
        ])
    ]
    for copy in local:
        copy.start()

    barrier = pltpu.get_barrier_semaphore()
    for k in range(1, n):
        pl.semaphore_signal(
            barrier, inc=1, device_id=(lax.rem(me + k, n), fs), device_id_type=MESH
        )
    pl.semaphore_signal(barrier, inc=1, device_id=(me, 1 - fs), device_id_type=MESH)
    taps[:, :rows] = jnp.zeros((group, rows), bf16)
    pl.semaphore_wait(barrier, n)

    pending = []

    def go(copy):
        copy.start()
        pending.append(copy)
        return copy

    own = wall.at[zi]
    x_copy = go(send(cot_ref, feat.at[fs], xsem.at[0], xsem.at[1], me, 1 - fs))
    go(send(wt_ref, own, wzs.at[1], wzr.at[1], at(1, 0)))
    go(send(wt_ref, own, wzs.at[2], wzr.at[2], at(2, 0)))

    def whole(src, dst, sems):
        others = pl.ds(0, n - 1)
        to = lax.rem(me + 1, n)
        return send(src.at[others], dst.at[others], sems.at[0], sems.at[1], to)

    def all_to_all(src, dst, sems):
        for k in range(1, n):
            to = lax.rem(me + k, n)
            send(src.at[to], dst.at[me], sems.at[0], sems.at[1], to).start()
        dst[me] = src[me]
        pending.append(whole(src, dst, sems))

    def arrive(src, dst, sems):
        whole(src, dst, sems).wait_recv()

    for copy in local:
        copy.wait()
    gated_all[q] = (gate_in[...].astype(f32) * conv_in[...].astype(f32)).astype(bf16)
    go(send(gated_all.at[q], gated_all.at[q], gts.at[2], gtr.at[2], at(0, 2)))
    go(send(gated_all.at[q], gated_all.at[q], gts.at[1], gtr.at[1], at(0, 1)))
    valt[...] = val_in[...].astype(f32).T.astype(bf16).reshape(n, group, rows)

    def weight_from(level):
        slot = wall.at[levels[level]]
        send(slot, slot, wzs.at[level], wzr.at[level], at(level, 0)).wait_recv()
        if level == 1:
            go(send(slot, slot, wzs.at[3], wzr.at[3], at(2, 0)))

    lane = lax.broadcasted_iota(jnp.int32, (n, group, rows), 2)

    def split(spec, re_ref, im_ref, mix_ref, sign):
        real = spec[:, :rows].reshape(n, group, rows)
        imag = spec[:, rows:].reshape(n, group, rows)
        re_ref[...] = real
        if mix_ref is None:
            im_ref[...] = imag
        else:
            im_ref[...] = jnp.where(lane == 0, 0.0, imag)
            mix_ref[...] = jnp.where(lane == 0, sign * imag, real)

    def spectra(source, re_ref, im_ref, mix_ref):
        blocks = source[...].reshape(n * group, rows)
        spec = jnp.dot(blocks, fwd_ref[:rows, :], preferred_element_type=f32)
        split(spec, re_ref, im_ref, mix_ref, 1.0)

    x_copy.wait_recv()
    for part in range(2):
        turned = feat[part].astype(f32).T.astype(bf16)
        per = turned.shape[0] // n * 2
        for j in range(n // 2):
            s = part * (n // 2) + j
            featq[s % 4, s // 4] = turned[j * per:(j + 1) * per]
    featr[q] = featq[q]
    for k in (2, 3, 1):
        go(send(featq.at[quad[k]], featr.at[q], fts.at[k], ftr.at[k], at(0, k)))
    weight_from(1)

    windows = jnp.concatenate(
        [taps[:, m * rows:(m + 2) * rows] for m in range(n)], axis=0
    )
    spec = jnp.dot(windows, fwd_ref[...], preferred_element_type=f32)
    split(spec, tre, tim, tmix, -1.0)

    for k in range(1, 4):
        send(featq.at[q], featr.at[quad[k]], fts.at[k], ftr.at[k], at(0, k)).wait_recv()
    slices, width = featr.shape[2], gated_all.shape[2]
    tokens = jnp.concatenate(
        [featr[k].reshape(nz * slices, rows) for k in range(4)], axis=1
    )
    weight_from(2)
    weight_from(3)
    partial = jnp.dot(
        tokens.astype(f32).T.astype(bf16),
        wall[...].reshape(nz * slices, width),
        preferred_element_type=f32,
    )
    for k in range(4):
        shares[k % 2, k // 2] = partial[k * rows:(k + 1) * rows]
    core_copy = go(send(shares.at[1 - core], core_in, ms.at[0], mr.at[0], at(0, 1)))

    far_gated = gated_all.at[quad[2]]
    send(far_gated, far_gated, gts.at[2], gtr.at[2], at(0, 2)).wait_recv()
    go(send(far_gated, far_gated, gts.at[3], gtr.at[3], at(0, 1)))

    core_copy.wait_recv()
    y_out[...] = (shares[core, 1 - y] + core_in[1 - y]).astype(bf16)
    y_copy = go(send(y_out, y_in, ms.at[1], mr.at[1], at(0, 2)))

    for k in (1, 3):
        there = gated_all.at[quad[k]]
        send(there, there, gts.at[k], gtr.at[k], at(0, k)).wait_recv()
    pw[...] = jnp.dot(
        tokens, gated_all[...].reshape(4 * rows, width), preferred_element_type=f32
    ).reshape(nz, slices, width)

    pair_out[0] = pw[levels[3]].astype(bf16)
    go(send(pair_out.at[0], pair_in.at[0], rs.at[0], rr.at[0], at(2, 0)))
    pair_out[1] = pw[levels[2]].astype(bf16)
    go(send(pair_out.at[1], pair_in.at[1], rs.at[1], rr.at[1], at(2, 0)))

    y_copy.wait_recv()
    mixed = shares[core, y] + core_in[y] + y_in[...].astype(f32)
    gct[...] = (mixed * gate_in[...].astype(f32)).T.astype(bf16).reshape(n, group, rows)
    all_to_all(gct, gcr, cs)
    gg_ref[...] = (mixed * conv_in[...].astype(f32)).astype(bf16)
    all_to_all(valt, valr, vs)

    arrive(gct, gcr, cs)
    spectra(gcr, cre, cim, None)
    send(pair_out.at[0], pair_in.at[0], rs.at[0], rr.at[0], at(2, 0)).wait_recv()
    cross_out[...] = (pw[levels[1]] + pair_in[0].astype(f32)).astype(bf16)
    go(send(cross_out, cross_in, rs.at[2], rr.at[2], at(1, 0)))

    block = 4

    def load(refs, j, at_rows):
        return tuple(ref[j, at_rows, :] for ref in refs)

    def value_rows(r, carry):
        at_rows = pl.ds(pl.multiple_of(r * 8, 8), 8)
        for base in range(0, n, block):
            real, imag, held = {}, {}, {}
            for j in range(base, n):
                c_re, c_im = load((cre, cim), j, at_rows)
                for i in range(base, min(base + block, j + 1)):
                    m = j - i
                    if m not in held:
                        held[m] = load((tre, tim, tmix), m, at_rows)
                    t_re, t_im, t_mix = held[m]
                    re, im = c_re * t_re + c_im * t_im, c_re * t_im - c_im * t_mix
                    real[i] = real[i] + re if i in real else re
                    imag[i] = imag[i] + im if i in imag else im
            for i in range(base, base + block):
                sums[i, at_rows, :rows] = real[i]
                sums[i, at_rows, rows:] = imag[i]
        return carry

    lax.fori_loop(0, group // 8, value_rows, 0)
    packed = sums[...].astype(bf16).reshape(n * group, 2 * rows)
    blocks = jnp.dot(packed, vback_ref[...], preferred_element_type=f32)
    gvt[...] = blocks.astype(bf16).reshape(n, group, rows)
    all_to_all(gvt, gvr, os)

    arrive(valt, valr, vs)
    spectra(valr, vre, vim, vmix)

    def lag_rows(r, carry):
        at_rows = pl.ds(pl.multiple_of(r * 8, 8), 8)
        for base in range(0, n, block):
            real, imag, held = {}, {}, {}
            for i in range(n - base):
                v_re, v_im, v_mix = load((vre, vim, vmix), i, at_rows)
                for m in range(base, min(base + block, n - i)):
                    j = i + m
                    if j not in held:
                        held[j] = load((cre, cim), j, at_rows)
                    c_re, c_im = held[j]
                    re, im = v_re * c_re + v_im * c_im, v_mix * c_im - v_im * c_re
                    real[m] = real[m] + re if m in real else re
                    imag[m] = imag[m] + im if m in imag else im
            for m in range(base, base + block):
                lags[m, at_rows, :rows] = real[m]
                lags[m, at_rows, rows:] = imag[m]
        return carry

    lax.fori_loop(0, group // 8, lag_rows, 0)
    packed = lags[...].astype(bf16).reshape(n * group, 2 * rows)
    parts = jnp.dot(packed, lback_ref[...], preferred_element_type=f32)
    first = jnp.concatenate([parts[group:, :rows], jnp.zeros((group, rows), f32)], axis=0)
    gft[...] = (parts[:, rows:] + first).astype(bf16).reshape(n, group, rows)
    all_to_all(gft, gfr, ls)

    send(pair_out.at[1], pair_in.at[1], rs.at[1], rr.at[1], at(2, 0)).wait_recv()
    send(cross_out, cross_in, rs.at[2], rr.at[2], at(1, 0)).wait_recv()
    gw_ref[...] = pw[zi] + pair_in[1].astype(f32) + cross_in[...].astype(f32)
    arrive(gvt, gvr, os)
    gv_ref[...] = gvr[...].reshape(n * group, rows)
    arrive(gft, gfr, ls)
    gf_ref[...] = gfr[...].reshape(n * group, rows)
    for copy in pending:
        copy.wait_send()


def finish_kernel(gv_ref, gg_ref, gf_ref, gw_ref, gv_out, gg_out, gf_out, gw_out):
    gv_out[...] = gv_ref[...].astype(jnp.float32).T.astype(jnp.bfloat16)
    gg_out[...] = gg_ref[...]
    gf_out[...] = gf_ref[...].astype(jnp.float32).T
    gw_out[...] = gw_ref[...]


def split_body(cotangent, out_weight, values, gate_input, conv_out, filter_taps):
    rows, channels = values.shape
    n = lax.axis_size("seq")
    nz = n // 4
    group = channels // n
    slice_cols = out_weight.shape[1]
    forward, value_back, lag_back = packed_tables(rows)
    bf16, f32 = jnp.bfloat16, jnp.float32
    vm = pltpu.VMEM
    dma = pltpu.SemaphoreType.DMA
    trip = (n, group, rows)
    vmem = pl.BlockSpec(memory_space=pltpu.VMEM)
    gv, gg, gf, gw = pl.pallas_call(
        functools.partial(mixer_kernel, n, nz),
        out_shape=(
            jax.ShapeDtypeStruct((channels, rows), bf16),
            jax.ShapeDtypeStruct((rows, channels), bf16),
            jax.ShapeDtypeStruct((channels, rows), bf16),
            jax.ShapeDtypeStruct((slice_cols, channels), f32),
        ),
        in_specs=[pl.BlockSpec(memory_space=pltpu.HBM)] * 9,
        out_specs=(vmem,) * 4,
        scratch_shapes=[vm((rows, channels), bf16)] * 3 + [
            vm((2 * rows, 2 * rows), bf16),
            vm((2 * rows, rows), bf16),
            vm((2 * rows, 2 * rows), bf16),
            vm((2, rows, channels), bf16),
            vm((nz, slice_cols, channels), bf16),
            vm((4, rows, channels), bf16),
            vm((4, nz, slice_cols, rows), bf16),
            vm((4, nz, slice_cols, rows), bf16),
        ] + [vm(trip, bf16)] * 8 + [
            vm((group, (n + 1) * rows), bf16),
        ] + [vm(trip, f32)] * 8 + [
            vm((n, group, 2 * rows), f32),
            vm((n, group, 2 * rows), f32),
            vm((nz, slice_cols, channels), f32),
            vm((2, slice_cols, channels), bf16),
            vm((2, slice_cols, channels), bf16),
            vm((slice_cols, channels), bf16),
            vm((slice_cols, channels), bf16),
            vm((2, 2, rows, channels), f32),
            vm((2, rows, channels), f32),
            vm((rows, channels), bf16),
            vm((rows, channels), bf16),
            dma((2,)),
            dma((nz,)), dma((nz,)), dma((2,)), dma((2,)),
            dma((4,)), dma((4,)), dma((4,)), dma((4,)),
        ] + [dma((2,))] * 4 + [dma((3,)), dma((3,)), dma((9,))],
        compiler_params=pltpu.CompilerParams(
            collective_id=0, has_side_effects=True, vmem_limit_bytes=60 * 1024 * 1024
        ),
    )(
        cotangent, out_weight.T, values, gate_input, conv_out, filter_taps,
        forward, value_back, lag_back,
    )
    gv, gg, gf, gw = pl.pallas_call(
        finish_kernel,
        out_shape=(
            jax.ShapeDtypeStruct((rows, channels), bf16),
            jax.ShapeDtypeStruct((rows, channels), bf16),
            jax.ShapeDtypeStruct((rows, channels), f32),
            jax.ShapeDtypeStruct((slice_cols, channels), f32),
        ),
        in_specs=[vmem] * 4,
        out_specs=(vmem,) * 4,
        compiler_params=pltpu.CompilerParams(vmem_limit_bytes=60 * 1024 * 1024),
    )(gv, gg, gf, gw)
    return gv, gg, gf, gw.T


def solution(mesh):
    in_specs = (
        P("seq", "fsdp"),
        P("fsdp", "seq"),
        P("seq", "fsdp"),
        P("seq", "fsdp"),
        P("seq", "fsdp"),
        P("fsdp", None),
    )
    out_specs = (P("seq", "fsdp"), P("seq", "fsdp"), P("seq", "fsdp"), P("fsdp", "seq"))

    def body(*blocks):
        rows, channels = blocks[2].shape
        n = mesh.shape["seq"]
        aligned = rows % 128 == 0 and channels % (16 * n) == 0 and blocks[1].shape[1] % 16 == 0
        if aligned and n == 16 and mesh.shape["fsdp"] == 2:
            return split_body(*blocks)
        return ring_body(*blocks)

    return jax.shard_map(body, mesh=mesh, in_specs=in_specs, out_specs=out_specs, check_vma=False)
```

```python
import functools

import jax
import jax.numpy as jnp
import numpy as np
from jax import lax
from jax.experimental import pallas as pl
from jax.experimental.pallas import tpu as pltpu
from jax.sharding import PartitionSpec as P

MESH = pl.DeviceIdType.MESH


def shifted(block, axis, distance):
    devices = range(lax.axis_size(axis))
    route = [(i - distance, i) for i in devices if i - distance in devices]
    return lax.ppermute(block, axis, route)


def make_tables(block_rows):
    period = 2 * block_rows
    frequency = lax.broadcasted_iota(jnp.int32, (period, period), 0)
    position = lax.broadcasted_iota(jnp.int32, (period, period), 1)
    angles = (frequency * position % period).astype(jnp.float32) * (2.0 * jnp.pi / period)
    cosine = jnp.cos(angles)
    sine_part = jnp.sin(angles)
    parity = 1.0 - 2.0 * (position % 2).astype(jnp.float32)
    dft_cos = cosine.astype(jnp.bfloat16)
    dft_sin = (-sine_part).astype(jnp.bfloat16)
    back_cos = (parity * cosine / period).astype(jnp.bfloat16)
    back_sin = (-parity * sine_part / period).astype(jnp.bfloat16)
    return (dft_cos, dft_sin, back_cos, back_sin)


def narrow_dot(left, right):
    return jnp.dot(left, right, preferred_element_type=jnp.float32)


def product_rows(table, window):
    return lax.dot_general(
        table, window, (((1,), (1,)), ((), ())), preferred_element_type=jnp.float32
    )


def spectrum(block, cos_part, sin_part):
    return (narrow_dot(cos_part, block), narrow_dot(sin_part, block))


def value_term(conv_re, conv_im, filt_re, filt_im, back_table):
    mixed_re = conv_re * filt_re + conv_im * filt_im
    mixed_im = conv_re * filt_im - conv_im * filt_re
    stacked = jnp.concatenate(
        [mixed_re.astype(jnp.bfloat16), mixed_im.astype(jnp.bfloat16)], axis=0
    )
    return narrow_dot(back_table, stacked)


def filter_term(val_re, val_im, conv_re, conv_im, back_table):
    mixed_re = val_re * conv_re + val_im * conv_im
    mixed_im = val_re * conv_im - val_im * conv_re
    stacked = jnp.concatenate(
        [mixed_re.astype(jnp.bfloat16), mixed_im.astype(jnp.bfloat16)], axis=0
    )
    return narrow_dot(back_table, stacked)


def ring_body(cotangent, out_weight, values, gate_input, conv_out, filter_taps):
    block_rows, channels = values.shape
    cycle_size = lax.axis_size("seq")
    weight_rows = lax.all_gather(out_weight, "seq", axis=1, tiled=True)
    features = lax.all_gather(cotangent, "fsdp", axis=1, tiled=True)
    grad_mixed = lax.dot_general(
        features, weight_rows, (((1,), (1,)), ((), ())), preferred_element_type=jnp.float32
    )
    gate_wide = gate_input.astype(jnp.float32)
    conv_wide = conv_out.astype(jnp.float32)
    grad_gate = (grad_mixed * conv_wide).astype(jnp.bfloat16)
    grad_conv = (grad_mixed * gate_wide).astype(jnp.bfloat16)
    gated = (gate_wide * conv_wide).astype(jnp.bfloat16)
    weight_terms = lax.dot_general(
        gated, features, (((0,), (0,)), ((), ())), preferred_element_type=jnp.float32
    )
    grad_weight = lax.psum_scatter(weight_terms, "seq", scatter_dimension=1, tiled=True)
    period = 2 * block_rows
    dft_cos, dft_sin, back_cos, back_sin = make_tables(block_rows)
    block_cos = dft_cos[:, :block_rows]
    block_sin = dft_sin[:, :block_rows]
    value_back = jnp.concatenate([back_cos[:block_rows], -back_sin[:block_rows]], axis=1)
    filter_back = jnp.concatenate([back_cos, back_sin], axis=1)
    padded_taps = jnp.concatenate(
        [jnp.zeros((channels, block_rows), jnp.bfloat16), filter_taps], axis=1
    )
    empty = jnp.zeros((block_rows, channels), jnp.float32)

    def window_spectrum(offset):
        window = lax.dynamic_slice_in_dim(padded_taps, offset * block_rows, period, 1)
        return (product_rows(dft_cos, window), product_rows(dft_sin, window))

    val_re, val_im = spectrum(values, block_cos, block_sin)

    def turn(offset, carry):
        incoming, grad_total, lag_grad = carry
        conv_re, conv_im = spectrum(incoming, block_cos, block_sin)
        filt_re, filt_im = window_spectrum(offset)
        grad_total = grad_total + value_term(conv_re, conv_im, filt_re, filt_im, value_back)
        start = offset * block_rows
        current = lax.dynamic_slice_in_dim(lag_grad, start, period, 0)
        update = current + filter_term(val_re, val_im, conv_re, conv_im, filter_back)
        lag_grad = lax.dynamic_update_slice_in_dim(lag_grad, update, start, 0)
        return (incoming, grad_total, lag_grad)

    def shifted_turn(offset, carry):
        incoming = shifted(carry[0], "seq", -1)
        return turn(offset, (incoming, carry[1], carry[2]))

    lag_zero = jnp.zeros(((cycle_size + 1) * block_rows, channels), jnp.float32)
    carry = turn(0, (grad_conv, empty, lag_zero))
    carry = lax.fori_loop(1, cycle_size, shifted_turn, carry)
    grad_total = carry[1]
    grad_filter = lax.psum_scatter(carry[2][block_rows:], "seq", scatter_dimension=0, tiled=True)
    return (grad_total.astype(jnp.bfloat16), grad_gate, grad_filter, grad_weight)


def packed_tables(rows):
    period = 2 * rows
    freq = np.arange(rows)
    pos = np.arange(period)
    angle = (np.outer(pos, freq) % period) * (2.0 * np.pi / period)
    cosine, sine = np.cos(angle), np.sin(angle)
    alternating = 1.0 - 2.0 * (pos % 2)
    forward_im = -sine
    forward_im[:, 0] = alternating
    forward = np.concatenate([cosine, forward_im], axis=1)
    parity = (1.0 - 2.0 * (freq % 2))[:, None]
    weight = np.where(freq == 0, 1.0, 2.0)[:, None] / period
    back_re = weight * parity * cosine.T
    value_im = weight * parity * sine.T
    lag_im = -value_im
    value_im[0] = alternating / period
    lag_im[0] = alternating / period
    value_back = np.concatenate([back_re, value_im], axis=0)[:, :rows]
    lag_back = np.concatenate([back_re, lag_im], axis=0)
    return tuple(jnp.asarray(t, jnp.bfloat16) for t in (forward, value_back, lag_back))


def mixer_kernel(
    n, nz,
    cot_ref, wt_ref, val_ref, gate_ref, conv_ref, taps_ref, fwd_hbm, vback_hbm, lback_hbm,
    gv_ref, gg_ref, gf_ref, gw_ref,
    val_in, gate_in, conv_in, fwd_ref, vback_ref, lback_ref,
    feat, wall, gated_all, featq, featr, valt, valr, gct, gcr, gvt, gvr, gft, gfr,
    taps, cre, cim, tre, tim, tmix, vre, vim, vmix, sums, lags, pw, pair_out, pair_in, cross_out, cross_in,
    shares, core_in, y_out, y_in,
    wzs, wzr, ms, mr, gts, gtr, fts, ftr, vs, cs, os, ls, rs, rr, tsem,
):
    rows = val_in.shape[0]
    group = gct.shape[1]
    bf16, f32 = jnp.bfloat16, jnp.float32
    me = lax.axis_index("seq")
    fs = lax.axis_index("fsdp")
    zi, q = me // 4, me % 4
    y, core = q // 2, q % 2
    quad = [
        (1 - y if k >= 2 else y) * 2 + (1 - core if k % 2 else core) for k in range(4)
    ]
    pair = zi + 1 - 2 * (zi % 2)
    cross = lax.rem(zi + 2, 4)
    far = lax.rem(pair + 2, 4)
    levels = [zi, cross, pair, far]

    def at(level, k):
        return levels[level] * 4 + quad[k]

    def send(src, dst, send_sem, recv_sem, seq, fsdp=None):
        return pltpu.make_async_remote_copy(
            src_ref=src, dst_ref=dst, send_sem=send_sem, recv_sem=recv_sem,
            device_id=(seq, fs if fsdp is None else fsdp), device_id_type=MESH,
        )

    local = [
        pltpu.make_async_copy(src, dst, tsem.at[i]) for i, (src, dst) in enumerate([
            (wt_ref, wall.at[zi]),
            (cot_ref, feat),
            (gate_ref, gate_in),
            (conv_ref, conv_in),
            (val_ref, val_in),
            (taps_ref.at[pl.ds(pl.multiple_of(me * group, group), group), :], taps.at[:, rows:]),
            (fwd_hbm, fwd_ref),
            (vback_hbm, vback_ref),
            (lback_hbm, lback_ref),
        ])
    ]
    for copy in local:
        copy.start()

    barrier = pltpu.get_barrier_semaphore()
    for k in range(1, n):
        pl.semaphore_signal(
            barrier, inc=1, device_id=(lax.rem(me + k, n), fs), device_id_type=MESH
        )
    for k in range(4):
        pl.semaphore_signal(barrier, inc=1, device_id=(at(0, k), 1 - fs), device_id_type=MESH)
    taps[:, :rows] = jnp.zeros((group, rows), bf16)
    pl.semaphore_wait(barrier, n + 3)

    pending = []

    def go(copy):
        copy.start()
        pending.append(copy)
        return copy

    own = wall.at[zi]
    go(send(wt_ref, own, wzs.at[1], wzr.at[1], at(1, 0)))
    go(send(wt_ref, own, wzs.at[2], wzr.at[2], at(2, 0)))

    def whole(src, dst, sems):
        others = pl.ds(0, n - 1)
        to = lax.rem(me + 1, n)
        return send(src.at[others], dst.at[others], sems.at[0], sems.at[1], to)

    def all_to_all(src, dst, sems):
        for k in range(1, n):
            to = lax.rem(me + k, n)
            send(src.at[to], dst.at[me], sems.at[0], sems.at[1], to).start()
        dst[me] = src[me]
        pending.append(whole(src, dst, sems))

    def arrive(src, dst, sems):
        whole(src, dst, sems).wait_recv()

    for copy in local:
        copy.wait()
    halves = nz // 2

    def feature_copy(k, dx):
        return send(
            featq.at[quad[k]], featr.at[q, pl.ds(fs * halves, halves)],
            fts.at[k + 4 * dx], ftr.at[k + 4 * dx], at(0, k), 1 - fs if dx else fs,
        )

    turned = feat[...].astype(f32).T.astype(bf16)
    per = turned.shape[0] * 2 // n
    for j in range(n // 2):
        featq[j % 4, j // 4] = turned[j * per:(j + 1) * per]
    for k, dx in ((2, 1), (3, 1), (2, 0), (3, 0), (0, 1), (1, 1), (1, 0)):
        go(feature_copy(k, dx))
    featr[q, pl.ds(fs * halves, halves)] = featq[q]
    gated_all[q] = (gate_in[...].astype(f32) * conv_in[...].astype(f32)).astype(bf16)
    go(send(gated_all.at[q], gated_all.at[q], gts.at[2], gtr.at[2], at(0, 2)))
    go(send(gated_all.at[q], gated_all.at[q], gts.at[1], gtr.at[1], at(0, 1)))
    valt[...] = val_in[...].astype(f32).T.astype(bf16).reshape(n, group, rows)

    def weight_from(level):
        slot = wall.at[levels[level]]
        send(slot, slot, wzs.at[level], wzr.at[level], at(level, 0)).wait_recv()
        if level == 1:
            go(send(slot, slot, wzs.at[3], wzr.at[3], at(2, 0)))

    lane = lax.broadcasted_iota(jnp.int32, (n, group, rows), 2)

    def split(spec, re_ref, im_ref, mix_ref, sign):
        real = spec[:, :rows].reshape(n, group, rows)
        imag = spec[:, rows:].reshape(n, group, rows)
        re_ref[...] = real
        if mix_ref is None:
            im_ref[...] = imag
        else:
            im_ref[...] = jnp.where(lane == 0, 0.0, imag)
            mix_ref[...] = jnp.where(lane == 0, sign * imag, real)

    def spectra(source, re_ref, im_ref, mix_ref):
        blocks = source[...].reshape(n * group, rows)
        spec = jnp.dot(blocks, fwd_ref[:rows, :], preferred_element_type=f32)
        split(spec, re_ref, im_ref, mix_ref, 1.0)

    weight_from(1)

    windows = jnp.concatenate(
        [taps[:, m * rows:(m + 2) * rows] for m in range(n)], axis=0
    )
    spec = jnp.dot(windows, fwd_ref[...], preferred_element_type=f32)
    split(spec, tre, tim, tmix, -1.0)

    for k, dx in ((1, 0), (2, 0), (3, 0), (0, 1), (1, 1), (2, 1), (3, 1)):
        half = 1 - fs if dx else fs
        send(
            featq.at[q], featr.at[quad[k], pl.ds(half * halves, halves)],
            fts.at[k + 4 * dx], ftr.at[k + 4 * dx], at(0, k), half,
        ).wait_recv()
    slices, width = featr.shape[2], gated_all.shape[2]
    tokens = jnp.concatenate(
        [featr[k].reshape(nz * slices, rows) for k in range(4)], axis=1
    )
    weight_from(2)
    weight_from(3)
    partial = jnp.dot(
        tokens.astype(f32).T.astype(bf16),
        wall[...].reshape(nz * slices, width),
        preferred_element_type=f32,
    )
    for k in range(4):
        shares[k % 2, k // 2] = partial[k * rows:(k + 1) * rows]
    core_copy = go(send(shares.at[1 - core], core_in, ms.at[0], mr.at[0], at(0, 1)))

    far_gated = gated_all.at[quad[2]]
    send(far_gated, far_gated, gts.at[2], gtr.at[2], at(0, 2)).wait_recv()
    go(send(far_gated, far_gated, gts.at[3], gtr.at[3], at(0, 1)))

    core_copy.wait_recv()
    y_out[...] = (shares[core, 1 - y] + core_in[1 - y]).astype(bf16)
    y_copy = go(send(y_out, y_in, ms.at[1], mr.at[1], at(0, 2)))

    for k in (1, 3):
        there = gated_all.at[quad[k]]
        send(there, there, gts.at[k], gtr.at[k], at(0, k)).wait_recv()
    pw[...] = jnp.dot(
        tokens, gated_all[...].reshape(4 * rows, width), preferred_element_type=f32
    ).reshape(nz, slices, width)

    pair_out[0] = pw[levels[3]].astype(bf16)
    go(send(pair_out.at[0], pair_in.at[0], rs.at[0], rr.at[0], at(2, 0)))
    pair_out[1] = pw[levels[2]].astype(bf16)
    go(send(pair_out.at[1], pair_in.at[1], rs.at[1], rr.at[1], at(2, 0)))

    y_copy.wait_recv()
    mixed = shares[core, y] + core_in[y] + y_in[...].astype(f32)
    gct[...] = (mixed * gate_in[...].astype(f32)).T.astype(bf16).reshape(n, group, rows)
    all_to_all(gct, gcr, cs)
    gg_ref[...] = (mixed * conv_in[...].astype(f32)).astype(bf16)
    all_to_all(valt, valr, vs)

    arrive(gct, gcr, cs)
    spectra(gcr, cre, cim, None)
    send(pair_out.at[0], pair_in.at[0], rs.at[0], rr.at[0], at(2, 0)).wait_recv()
    cross_out[...] = (pw[levels[1]] + pair_in[0].astype(f32)).astype(bf16)
    go(send(cross_out, cross_in, rs.at[2], rr.at[2], at(1, 0)))

    block = 4

    def load(refs, j, at_rows):
        return tuple(ref[j, at_rows, :] for ref in refs)

    def value_rows(r, carry):
        at_rows = pl.ds(pl.multiple_of(r * 8, 8), 8)
        for base in range(0, n, block):
            real, imag, held = {}, {}, {}
            for j in range(base, n):
                c_re, c_im = load((cre, cim), j, at_rows)
                for i in range(base, min(base + block, j + 1)):
                    m = j - i
                    if m not in held:
                        held[m] = load((tre, tim, tmix), m, at_rows)
                    t_re, t_im, t_mix = held[m]
                    re, im = c_re * t_re + c_im * t_im, c_re * t_im - c_im * t_mix
                    real[i] = real[i] + re if i in real else re
                    imag[i] = imag[i] + im if i in imag else im
            for i in range(base, base + block):
                sums[i, at_rows, :rows] = real[i]
                sums[i, at_rows, rows:] = imag[i]
        return carry

    lax.fori_loop(0, group // 8, value_rows, 0)
    packed = sums[...].astype(bf16).reshape(n * group, 2 * rows)
    blocks = jnp.dot(packed, vback_ref[...], preferred_element_type=f32)
    gvt[...] = blocks.astype(bf16).reshape(n, group, rows)
    all_to_all(gvt, gvr, os)

    arrive(valt, valr, vs)
    spectra(valr, vre, vim, vmix)

    def lag_rows(r, carry):
        at_rows = pl.ds(pl.multiple_of(r * 8, 8), 8)
        for base in range(0, n, block):
            real, imag, held = {}, {}, {}
            for i in range(n - base):
                v_re, v_im, v_mix = load((vre, vim, vmix), i, at_rows)
                for m in range(base, min(base + block, n - i)):
                    j = i + m
                    if j not in held:
                        held[j] = load((cre, cim), j, at_rows)
                    c_re, c_im = held[j]
                    re, im = v_re * c_re + v_im * c_im, v_mix * c_im - v_im * c_re
                    real[m] = real[m] + re if m in real else re
                    imag[m] = imag[m] + im if m in imag else im
            for m in range(base, base + block):
                lags[m, at_rows, :rows] = real[m]
                lags[m, at_rows, rows:] = imag[m]
        return carry

    lax.fori_loop(0, group // 8, lag_rows, 0)
    packed = lags[...].astype(bf16).reshape(n * group, 2 * rows)
    parts = jnp.dot(packed, lback_ref[...], preferred_element_type=f32)
    first = jnp.concatenate([parts[group:, :rows], jnp.zeros((group, rows), f32)], axis=0)
    gft[...] = (parts[:, rows:] + first).astype(bf16).reshape(n, group, rows)
    all_to_all(gft, gfr, ls)

    send(pair_out.at[1], pair_in.at[1], rs.at[1], rr.at[1], at(2, 0)).wait_recv()
    send(cross_out, cross_in, rs.at[2], rr.at[2], at(1, 0)).wait_recv()
    gw_ref[...] = pw[zi] + pair_in[1].astype(f32) + cross_in[...].astype(f32)
    arrive(gvt, gvr, os)
    gv_ref[...] = gvr[...].reshape(n * group, rows)
    arrive(gft, gfr, ls)
    gf_ref[...] = gfr[...].reshape(n * group, rows)
    for copy in pending:
        copy.wait_send()


def finish_kernel(gv_ref, gg_ref, gf_ref, gw_ref, gv_out, gg_out, gf_out, gw_out):
    gv_out[...] = gv_ref[...].astype(jnp.float32).T.astype(jnp.bfloat16)
    gg_out[...] = gg_ref[...]
    gf_out[...] = gf_ref[...].astype(jnp.float32).T
    gw_out[...] = gw_ref[...]


def split_body(cotangent, out_weight, values, gate_input, conv_out, filter_taps):
    rows, channels = values.shape
    n = lax.axis_size("seq")
    nz = n // 4
    group = channels // n
    slice_cols = out_weight.shape[1]
    forward, value_back, lag_back = packed_tables(rows)
    bf16, f32 = jnp.bfloat16, jnp.float32
    vm = pltpu.VMEM
    dma = pltpu.SemaphoreType.DMA
    trip = (n, group, rows)
    vmem = pl.BlockSpec(memory_space=pltpu.VMEM)
    gv, gg, gf, gw = pl.pallas_call(
        functools.partial(mixer_kernel, n, nz),
        out_shape=(
            jax.ShapeDtypeStruct((channels, rows), bf16),
            jax.ShapeDtypeStruct((rows, channels), bf16),
            jax.ShapeDtypeStruct((channels, rows), bf16),
            jax.ShapeDtypeStruct((slice_cols, channels), f32),
        ),
        in_specs=[pl.BlockSpec(memory_space=pltpu.HBM)] * 9,
        out_specs=(vmem,) * 4,
        scratch_shapes=[vm((rows, channels), bf16)] * 3 + [
            vm((2 * rows, 2 * rows), bf16),
            vm((2 * rows, rows), bf16),
            vm((2 * rows, 2 * rows), bf16),
            vm((rows, channels), bf16),
            vm((nz, slice_cols, channels), bf16),
            vm((4, rows, channels), bf16),
            vm((4, nz // 2, slice_cols, rows), bf16),
            vm((4, nz, slice_cols, rows), bf16),
        ] + [vm(trip, bf16)] * 8 + [
            vm((group, (n + 1) * rows), bf16),
        ] + [vm(trip, f32)] * 8 + [
            vm((n, group, 2 * rows), f32),
            vm((n, group, 2 * rows), f32),
            vm((nz, slice_cols, channels), f32),
            vm((2, slice_cols, channels), bf16),
            vm((2, slice_cols, channels), bf16),
            vm((slice_cols, channels), bf16),
            vm((slice_cols, channels), bf16),
            vm((2, 2, rows, channels), f32),
            vm((2, rows, channels), f32),
            vm((rows, channels), bf16),
            vm((rows, channels), bf16),
            dma((nz,)), dma((nz,)), dma((2,)), dma((2,)),
            dma((4,)), dma((4,)), dma((8,)), dma((8,)),
        ] + [dma((2,))] * 4 + [dma((3,)), dma((3,)), dma((9,))],
        compiler_params=pltpu.CompilerParams(
            collective_id=0, has_side_effects=True, vmem_limit_bytes=60 * 1024 * 1024
        ),
    )(
        cotangent, out_weight.T, values, gate_input, conv_out, filter_taps,
        forward, value_back, lag_back,
    )
    gv, gg, gf, gw = pl.pallas_call(
        finish_kernel,
        out_shape=(
            jax.ShapeDtypeStruct((rows, channels), bf16),
            jax.ShapeDtypeStruct((rows, channels), bf16),
            jax.ShapeDtypeStruct((rows, channels), f32),
            jax.ShapeDtypeStruct((slice_cols, channels), f32),
        ),
        in_specs=[vmem] * 4,
        out_specs=(vmem,) * 4,
        compiler_params=pltpu.CompilerParams(vmem_limit_bytes=60 * 1024 * 1024),
    )(gv, gg, gf, gw)
    return gv, gg, gf, gw.T


def solution(mesh):
    in_specs = (
        P("seq", "fsdp"),
        P("fsdp", "seq"),
        P("seq", "fsdp"),
        P("seq", "fsdp"),
        P("seq", "fsdp"),
        P("fsdp", None),
    )
    out_specs = (P("seq", "fsdp"), P("seq", "fsdp"), P("seq", "fsdp"), P("fsdp", "seq"))

    def body(*blocks):
        rows, channels = blocks[2].shape
        n = mesh.shape["seq"]
        aligned = rows % 128 == 0 and channels % (16 * n) == 0 and blocks[1].shape[1] % 16 == 0
        if aligned and n == 16 and mesh.shape["fsdp"] == 2:
            return split_body(*blocks)
        return ring_body(*blocks)

    return jax.shard_map(body, mesh=mesh, in_specs=in_specs, out_specs=out_specs, check_vma=False)
```
